128 devices in a mesh: section: 4 (over x), head: 32 (over y, z, core).
Axes of the slice: x: 4, y: 4, z: 4, core: 2. Of those that a mesh axis runs over, the one named last changes fastest.
Arguments:
- token_ids: int32 [2, 12, 5], replicated, may hold values from 0 to 65535
- accepted: int32 [2, 12], replicated, may hold values from 1 to 5, 36 in all within a row
- embedding: bfloat16 [65536, 4096], P('section', 'head'), may hold values from -6 to 6
- norm_gain: float32 [4, 4096], P('section'), may hold values from 0.5 to 1.5
- w_gate: bfloat16 [4, 4096, 8192], P('section', None, 'head'), may hold values from -0.09375 to 0.09375
- w_input: bfloat16 [4, 4096, 8192], P('section', None, 'head'), may hold values from -0.09375 to 0.09375
- w_groups: bfloat16 [4, 4096, 2048], P('section', None, 'head'), may hold values from -0.046875 to 0.046875
- w_step: bfloat16 [4, 4096, 128], P('section', None, 'head'), may hold values from -0.09375 to 0.09375
- step_bias: float32 [4, 128], P('section', 'head'), may hold values from -4 to 1
- decay_rate: float32 [4, 128], P('section', 'head'), may hold values from 0.02 to 4
- skip_gain: float32 [4, 128], P('section', 'head'), may hold values from 0.5 to 1.5
- w_output: bfloat16 [4, 8192, 4096], P('section', 'head'), may hold values from -0.0625 to 0.0625
- states: bfloat16 [4, 12, 128, 64, 128], P('section', None, 'head'), may hold values from -4 to 4
- draft_gain: float32 [4096], replicated, may hold values from 0.5 to 1.5
- w_merge: bfloat16 [8192, 4096], P('section', 'head'), may hold values from -0.0625 to 0.0625
Outputs:
- kept_states: bfloat16 [4, 12, 128, 64, 128], P('section', None, 'head')
- draft_features: bfloat16 [72, 4096], P('section', 'head')
The draws below stay inside these ranges and needn't reach their ends.
Inputs may be any that keep to these rules, and one draw needn't show every extreme that they name: accepted[r, b] is the count of one row b in one round r, between 1 and 5. For each round r, the 12 counts accepted[r, 0] .. accepted[r, 11] together sum to 36, and in each round at least one row keeps all 5 positions.
All inputs are finite; a program needn't handle non-finite values.
Results may differ from the reference program's by a relative error of at most 0.035.
Values may be sent and summed in bfloat16 or wider, within the bound.
No kernel may reach another device: no remote copies, remote signals or barrier semaphores. Data moves between devices by JAX's collectives and lax.ppermute only.
A program may use at most 128 MiB of HBM per device.

```python
import math
import jax
import jax.numpy as jnp
import numpy as np
from jax import lax

D = 4096
HEAD_DIM = 64
STATE = 128
GROUPS = 8
VOCAB = 65536
POS = 5
ROWS = 12
HEADS = 128
INNER = 8192
ACCEPTED = 36
N_SECTION = 4


def touch_ends(values, stream_key, low, top_value):
    extent = values.shape
    place = [jax.random.randint(jax.random.fold_in(stream_key, axis), (), 0, extent[axis]) for axis in range(len(extent))]
    values = values.at[tuple(place)].set(low)
    longest = extent.index(max(extent))
    place[longest] = (place[longest] + 1) % extent[longest]
    return values.at[tuple(place)].set(top_value)


def steps_of(key, dims, split, least, largest):
    loudness, own = 1.0, jax.random.fold_in(key, 6)
    for dim, shards_of in split:
        heights = jnp.exp(jax.random.uniform(jax.random.fold_in(own, dim), (shards_of,), jnp.float32, least / len(split), largest / len(split)))
        loudness = loudness * jnp.repeat(heights, dims[dim] // shards_of).reshape([-1 if axis == dim else 1 for axis in range(len(dims))])
    return loudness


def split_up(count, total, limit, skew):
    loads = [(1 << 20) // math.isqrt(grade ** skew) + 1 for grade in range(2, count + 1)]
    spare, given = total - limit - (count - 1), [1] * (count - 1)
    while spare > 0:
        movable = [i for i in range(count - 1) if given[i] < limit]
        mass, left = sum([loads[i] for i in movable]), spare
        for i in movable:
            extra = min(limit - given[i], max(1, left * loads[i] // mass), spare)
            given[i] = given[i] + extra
            spare = spare - extra
    return np.array([limit] + given)


def uneven(rng, count, total, reach, slope):
    if count == 2:
        one = jax.random.randint(rng, (), max(1, total - reach), min(reach, total - 1) + 1)
        return jnp.stack([one, total - one])
    tallies = jnp.asarray(split_up(count, total, reach, slope), jnp.int32)
    twos = (count - 1) // 2
    source_of, sink = tallies[1:1 + 2 * twos:2], tallies[2:2 + 2 * twos:2]
    margin = jnp.minimum(source_of - 1, reach - sink)
    passed = jax.random.randint(jax.random.fold_in(rng, 1), (twos,), 0, 1 << 20) % (margin + 1)
    tallies = tallies.at[1:1 + 2 * twos:2].set(source_of - passed).at[2:2 + 2 * twos:2].set(sink + passed)
    return tallies[jax.random.permutation(jax.random.fold_in(rng, 2), count)]


def normal_values(rng, shape, width, bound, cuts=(), kind=jnp.bfloat16):
    loudness = steps_of(rng, shape, cuts, -0.22, 0.18) if cuts else 1.0
    drawn = jax.random.normal(rng, shape, jnp.float32) * width * loudness
    return jnp.minimum(jnp.maximum(drawn, -bound), bound).astype(kind)


def setup_inputs(seed: int = 0) -> dict:
    keys = jax.random.split(jax.random.key(seed), 16)
    return {
        "token_ids": touch_ends(jax.random.randint(keys[0], (2, ROWS, POS), 0, VOCAB), jax.random.fold_in(keys[0], 1), 0, VOCAB - 1).astype(jnp.int32),
        "accepted": jax.vmap(lambda own: uneven(own, ROWS, ACCEPTED, POS, 2))(jax.random.split(keys[1], 2)).reshape((2, ROWS)).astype(jnp.int32),
        "embedding": normal_values(keys[2], (VOCAB, D), 1.0, 6.0, ((0, 4), (1, 32))),
        "norm_gain": jnp.clip(1.0 + 0.1 * jax.random.normal(keys[3], (N_SECTION, D), jnp.float32), 0.5, 1.5),
        "w_gate": normal_values(keys[4], (N_SECTION, D, INNER), D ** -0.5, 0.09375, ((0, 4), (2, 32))),
        "w_input": normal_values(keys[5], (N_SECTION, D, INNER), D ** -0.5, 0.09375, ((0, 4), (2, 32))),
        "w_groups": normal_values(keys[6], (N_SECTION, D, 2 * GROUPS * STATE), (4 * D) ** -0.5, 0.046875, ((0, 4), (2, 32))),
        "w_step": normal_values(keys[7], (N_SECTION, D, HEADS), D ** -0.5, 0.09375, ((0, 4), (2, 32))),
        "step_bias": jnp.clip(-4.0 + 5.0 * jax.random.uniform(keys[8], (N_SECTION, HEADS), jnp.float32) ** steps_of(keys[8], (N_SECTION, HEADS), ((0, 4), (1, 32)), -0.2, 0.2), -4.0, 1.0),
        "decay_rate": jnp.clip(jnp.exp(math.log(4.0) - 5.2983174 * jax.random.uniform(keys[9], (N_SECTION, HEADS), jnp.float32) ** steps_of(keys[9], (N_SECTION, HEADS), ((0, 4), (1, 32)), -0.2, 0.2)), 0.02, 4.0),
        "skip_gain": jnp.clip(0.5 + 1.0 * jax.random.uniform(keys[10], (N_SECTION, HEADS), jnp.float32) ** steps_of(keys[10], (N_SECTION, HEADS), ((0, 4), (1, 32)), -0.2, 0.2), 0.5, 1.5),
        "w_output": normal_values(keys[11], (N_SECTION, INNER, D), INNER ** -0.5, 0.0625, ((0, 4), (1, 32))),
        "states": normal_values(keys[12], (N_SECTION, ROWS, HEADS, HEAD_DIM, STATE), 0.3, 4.0, ((0, 4), (2, 32))),
        "draft_gain": jnp.clip(1.0 + 0.1 * jax.random.normal(keys[13], (D,), jnp.float32), 0.5, 1.5),
        "w_merge": normal_values(keys[14], (2 * D, D), (2 * D) ** -0.5, 0.0625, ((0, 4), (1, 32))),
    }


epsilon = 1e-05

def rms_scale(values, norm_scale):
    values_f32 = values.astype(jnp.float32)
    return values_f32 * lax.rsqrt(lax.optimization_barrier(jnp.mean(values_f32 * values_f32, axis=-1, keepdims=True)) + epsilon) * norm_scale

def pack_order(accepted, positions):
    row_count = accepted.shape[1]
    ends = jnp.cumsum(accepted, axis=1).astype(jnp.int32)
    starts = ends - accepted
    slots = jnp.arange(ACCEPTED, dtype=jnp.int32)
    owner = lax.optimization_barrier(jnp.sum((slots[None, :, None] >= ends[:, None, :]).astype(jnp.int32), axis=2)).astype(jnp.int32)
    picked = owner[:, :, None] == jnp.arange(row_count, dtype=jnp.int32)[None, None, :]
    offsets = lax.optimization_barrier(jnp.sum(jnp.where(picked, starts[:, None, :], 0), axis=2)).astype(jnp.int32)
    rounds = jnp.arange(2, dtype=jnp.int32)[:, None] * (row_count * positions)
    return (owner * positions + slots[None, :] - offsets + rounds).reshape(-1).astype(jnp.int32)

def mixer(hidden, layer_state, counts, norm_scale, w_gate, w_input, w_groups, w_step, step_bias, decay_rate, skip_gain, w_output):
    normed = rms_scale(hidden, norm_scale).astype(jnp.bfloat16)
    gate_proj = jnp.dot(normed, w_gate, preferred_element_type=jnp.float32)
    inner_proj = jnp.dot(normed, w_input, preferred_element_type=jnp.float32)
    group_part = jnp.dot(normed, w_groups, preferred_element_type=jnp.float32).astype(jnp.bfloat16)
    group_part = lax.optimization_barrier(group_part).astype(jnp.float32)
    step_size = jax.nn.softplus(jnp.dot(normed, w_step, preferred_element_type=jnp.float32) + step_bias)
    row_count = layer_state.shape[0]
    heads_all = layer_state.shape[1]
    inner = inner_proj.reshape(row_count, POS, heads_all, HEAD_DIM)
    step_size = step_size.reshape(row_count, POS, heads_all)
    groups_rows = jnp.transpose(group_part.reshape(row_count, POS, STATE, 2, GROUPS), (0, 1, 4, 3, 2))
    per_head = jnp.repeat(groups_rows, heads_all // GROUPS, axis=2)
    decay = jnp.exp(-step_size * decay_rate)
    carried = layer_state.astype(jnp.float32)
    kept_state = jnp.zeros_like(carried)
    outputs = []
    for position in range(POS):
        carried = decay[:, position, :, None, None] * carried + (step_size[:, position, :, None] * inner[:, position])[:, :, :, None] * per_head[:, position, :, 0][:, :, None, :]
        read_out = jnp.einsum('bhpn,bhn->bhp', carried, per_head[:, position, :, 1], precision=lax.Precision.HIGHEST)
        outputs.append(read_out + skip_gain[None, :, None] * inner[:, position])
        kept_state = jnp.where((counts == position + 1)[:, None, None, None], carried, kept_state)
    mixed_out = jnp.stack(outputs, axis=1).reshape(row_count * POS, heads_all * HEAD_DIM)
    gated = (mixed_out * jax.nn.silu(gate_proj)).astype(jnp.bfloat16)
    result = (hidden.astype(jnp.float32) + jnp.dot(gated, w_output, preferred_element_type=jnp.float32)).astype(jnp.bfloat16)
    return (result, kept_state.astype(jnp.bfloat16))

def reference(token_ids, accepted, embedding, norm_gain, w_gate, w_input, w_groups, w_step, step_bias, decay_rate, skip_gain, w_output, states, draft_gain, w_merge):
    embedded = jnp.take(embedding, token_ids.reshape(-1), axis=0).reshape(2, ROWS * POS, D)
    layer_states = [states[layer] for layer in range(N_SECTION)]
    finals = []
    for round_index in range(2):
        hidden = embedded[round_index]
        for layer in range(N_SECTION):
            hidden, layer_states[layer] = mixer(hidden, layer_states[layer], accepted[round_index], norm_gain[layer], w_gate[layer], w_input[layer], w_groups[layer], w_step[layer], step_bias[layer], decay_rate[layer], skip_gain[layer], w_output[layer])
        finals.append(hidden)
    order = pack_order(accepted, POS)
    chosen = jnp.take(jnp.concatenate(finals, axis=0), order, axis=0)
    normed = rms_scale(chosen, draft_gain).astype(jnp.bfloat16)
    tokens_packed = jnp.take(embedded.reshape(2 * ROWS * POS, D), order, axis=0)
    joined = jnp.concatenate([normed, tokens_packed], axis=1)
    draft_out = jnp.dot(joined, w_merge, preferred_element_type=jnp.float32).astype(jnp.bfloat16)
    return (jnp.stack(layer_states), draft_out)
```

```python
import functools

import jax
import jax.numpy as jnp
from jax import lax
from jax.experimental import pallas as pl
from jax.experimental.pallas import tpu as pltpu
from jax.sharding import PartitionSpec as P

HEAD_DIM = 64
STATE = 128
GROUPS = 8
ACCEPTED = 36
POS = 5
ROWS = 12
PACKED = 2 * ACCEPTED
SLOTS = 80
WIDTH = 4096
CHUNK = 512
CELL = 128

epsilon = 1e-05
bf16 = jnp.bfloat16
f32 = jnp.float32

VMEM = pl.BlockSpec(memory_space=pltpu.VMEM)
SMEM = pl.BlockSpec(memory_space=pltpu.SMEM)
NT = (((1,), (1,)), ((), ()))
TN = (((0,), (0,)), ((), ()))


def route(value, target):
    pairs = []
    for source in range(128):
        x, y, z, c = target(source >> 5, (source >> 3) & 3, (source >> 1) & 3, source & 1)
        pairs.append((source, ((x & 3) << 5) | (y << 3) | (z << 1) | c))
    return lax.ppermute(value, ("section", "head"), pairs)


def over_core(value):
    return route(value, lambda x, y, z, c: (x, y, z, c ^ 1))


def over_z(value, e):
    return route(value, lambda x, y, z, c: (x, y, z ^ e, c))


def over_y(value, d):
    return route(value, lambda x, y, z, c: (x, y ^ d, z, c))


def over_x(value, s):
    return route(value, lambda x, y, z, c: (x ^ s, y, z, c))


def next_section(value, d):
    return route(value, lambda x, y, z, c: (x + 1, y ^ d, z, c))


def ends_of(accepted_ref):
    ends = []
    for r in range(2):
        total = 0
        row = []
        for b in range(ROWS):
            total = total + accepted_ref[r, b]
            row.append(total)
        ends.append(row)
    return ends


def owner_of(ends, slot):
    later = slot >= ACCEPTED
    inner = jnp.where(later, slot - ACCEPTED, slot)
    owner = jnp.zeros_like(slot)
    for b in range(ROWS):
        end = jnp.where(later, ends[1][b], ends[0][b])
        owner = owner + (inner >= end).astype(jnp.int32)
    return owner


def pick_kernel(accepted_ref, own_ref, a_ref, b_ref, c_ref, out_ref):
    ends = ends_of(accepted_ref)
    lane = lax.broadcasted_iota(jnp.int32, (1, 2 * ROWS * POS), 1)
    slot_of = jnp.full((1, 2 * ROWS * POS), -1, jnp.int32)
    for r in range(2):
        for b in range(ROWS):
            low = (r * ROWS + b) * POS
            count = accepted_ref[r, b]
            start = ends[r][b] - count + r * ACCEPTED
            here = (lane >= low) & (lane < low + count)
            slot_of = jnp.where(here, start + lane - low, slot_of)
    slot = lax.broadcasted_iota(jnp.int32, (SLOTS, 2 * ROWS * POS), 0)
    picked = (slot == slot_of).astype(bf16)
    rows = (
        own_ref[...].astype(f32)
        + a_ref[...].astype(f32)
        + b_ref[...].astype(f32)
        + c_ref[...].astype(f32)
    ).astype(bf16)
    out_ref[...] = jnp.dot(picked, rows, preferred_element_type=f32).astype(bf16)


def softplus(v):
    return jnp.maximum(v, 0.0) + jnp.log1p(jnp.exp(-jnp.abs(v)))


def fill_hidden(first, y, z, c, pieces, hidden):
    total = jnp.zeros((SLOTS, CELL), f32)
    for f in range(2):
        for e in range(4):
            piece = pieces[f * 4 + e]
            if first:
                for d in range(4):
                    place = ((y ^ d) * 4 + (z ^ e)) * 2 + (c ^ f)
                    part = piece[d]
                    hidden[:, pl.ds(pl.multiple_of(place * CELL, CELL), CELL)] = part
                    wide = part.astype(f32)
                    total = total + wide * wide
            else:
                place = (c ^ f) * 4 + (z ^ e)
                part = piece[...]
                hidden[:, pl.ds(pl.multiple_of(place * CHUNK, CHUNK), CHUNK)] = part
                wide = part.astype(f32)
                square = wide * wide
                for i in range(CHUNK // CELL):
                    total = total + square[:, i * CELL : (i + 1) * CELL]
    return jnp.sum(total, axis=1, keepdims=True)


def layer_kernel(first, tick, *refs):
    (accepted_ref, idx_ref, bias_ref, rate_ref, skip_ref) = refs[:5]
    pieces = refs[5:13]
    (gain_ref, w_gate, w_input, w_pairs, w_step, w_output, states, place_ref) = refs[13:21]
    refs = refs[21:]
    if not first:
        old_x, old_b, old_decay = refs[:3]
        refs = refs[3:]
    kept_ref, sent_ref, new_x, new_b, new_decay, hidden, normed = refs
    y, z, c = idx_ref[1], idx_ref[2], idx_ref[3]
    ends = ends_of(accepted_ref)

    squares = fill_hidden(first, y, z, c, pieces, hidden)
    scale = lax.rsqrt(squares * (1.0 / WIDTH) + epsilon)
    for i in range(WIDTH // CHUNK):
        at = slice(i * CHUNK, (i + 1) * CHUNK)
        normed[:, at] = (hidden[:, at].astype(f32) * scale * gain_ref[:, at]).astype(bf16)
    rows = normed[...]
    gate = jnp.dot(rows, w_gate[...], preferred_element_type=f32)
    inner = jnp.dot(rows, w_input[...], preferred_element_type=f32)
    pairs = lax.dot_general(rows, w_pairs[...], NT, preferred_element_type=f32).astype(bf16)
    pairs = jnp.dot(pairs, place_ref[...], preferred_element_type=f32).astype(bf16)
    b_vec, c_vec = pairs[:, :STATE], pairs[:, STATE:]
    raw = lax.dot_general(rows, w_step[...], NT, preferred_element_type=f32)

    lane = lax.broadcasted_iota(jnp.int32, (1, 16), 1)
    bias = jnp.zeros((1, 16), f32)
    rate = jnp.zeros((1, 16), f32)
    for h in range(4):
        bias = jnp.where(lane == h, bias_ref[0, h], bias)
        rate = jnp.where(lane == h, rate_ref[0, h], rate)
    step = softplus(raw + bias)
    fall = step * rate

    row_owner = owner_of(ends, lax.broadcasted_iota(jnp.int32, (SLOTS, SLOTS), 0))
    col_owner = owner_of(ends, lax.broadcasted_iota(jnp.int32, (SLOTS, SLOTS), 1))
    same = row_owner == col_owner
    ahead = lax.broadcasted_iota(jnp.int32, (SLOTS, SLOTS), 1) <= lax.broadcasted_iota(
        jnp.int32, (SLOTS, SLOTS), 0
    )
    causal = same & ahead
    causal_f32 = causal.astype(f32)
    log_decay = -jnp.dot(
        causal_f32, fall, precision=lax.Precision.HIGHEST, preferred_element_type=f32
    )
    log_decay_t = -lax.dot_general(
        fall,
        causal_f32,
        (((0,), (1,)), ((), ())),
        precision=lax.Precision.HIGHEST,
        preferred_element_type=f32,
    )
    after = (same & jnp.logical_not(ahead)).astype(f32)
    rest = -jnp.dot(after, fall, precision=lax.Precision.HIGHEST, preferred_element_type=f32)
    batch = lax.broadcasted_iota(jnp.int32, (16, SLOTS), 0)
    batch_owner = owner_of(ends, lax.broadcasted_iota(jnp.int32, (16, SLOTS), 1))
    total = -jnp.dot(
        (batch == batch_owner).astype(f32),
        fall,
        precision=lax.Precision.HIGHEST,
        preferred_element_type=f32,
    )

    products = lax.dot_general(c_vec, b_vec, NT, preferred_element_type=f32)
    slot_owner = owner_of(ends, lax.broadcasted_iota(jnp.int32, (SLOTS, STATE), 0))
    carried = jnp.zeros((SLOTS, 4 * HEAD_DIM), f32)
    for b in range(ROWS):
        mine = jnp.where(slot_owner == b, c_vec, jnp.zeros((), bf16))
        carried = carried + lax.dot_general(mine, states[b], NT, preferred_element_type=f32)

    wide_lane = lax.broadcasted_iota(jnp.int32, (SLOTS, 2 * HEAD_DIM), 1)
    left = wide_lane < HEAD_DIM

    def spread(v, p):
        return jnp.where(left, v[:, 2 * p : 2 * p + 1], v[:, 2 * p + 1 : 2 * p + 2])

    gated = []
    weighted = []
    for p in range(2):
        at = slice(p * 128, (p + 1) * 128)
        x_p = inner[:, at]
        dx = spread(step, p) * x_p
        dx_b = dx.astype(bf16)
        mixed = []
        for h in (2 * p, 2 * p + 1):
            gap = log_decay[:, h : h + 1] - log_decay_t[h : h + 1, :]
            weights = products * jnp.exp(jnp.where(causal, gap, -1e30))
            mixed.append(jnp.dot(weights.astype(bf16), dx_b, preferred_element_type=f32))
        out = jnp.where(left, mixed[0], mixed[1])
        out = out + jnp.exp(spread(log_decay, p)) * carried[:, at]
        skip = jnp.where(left, skip_ref[0, 2 * p], skip_ref[0, 2 * p + 1])
        out = out + skip * x_p
        g = gate[:, at]
        gated.append((out * (g / (1.0 + jnp.exp(-g)))).astype(bf16))
        weighted.append((jnp.exp(spread(rest, p)) * dx).astype(bf16))
    gated = jnp.concatenate(gated, axis=1)

    for f in range(2):
        for e in range(4):
            place = (c ^ f) * 4 + (z ^ e)
            w = w_output[:, pl.ds(pl.multiple_of(place * CHUNK, CHUNK), CHUNK)]
            part = jnp.dot(gated, w, preferred_element_type=f32)
            if f == 0 and e == 0:
                own = hidden[:, pl.ds(pl.multiple_of(place * CHUNK, CHUNK), CHUNK)]
                kept_ref[e] = part + jnp.where(y == 0, own.astype(f32), 0.0)
            elif f == 0:
                kept_ref[e] = part
            else:
                sent_ref[e] = part.astype(bf16)

    decay = jnp.exp(total)
    if first:
        new_x[:, :128] = weighted[0]
        new_x[:, 128:] = weighted[1]
        new_b[...] = b_vec
        new_decay[...] = decay
    else:
        now = idx_ref[0] == tick
        new_x[:, :128] = jnp.where(now, weighted[0], old_x[:, :128])
        new_x[:, 128:] = jnp.where(now, weighted[1], old_x[:, 128:])
        new_b[...] = jnp.where(now, b_vec, old_b[...])
        new_decay[...] = jnp.where(now, decay, old_decay[...])


def state_kernel(accepted_ref, x_ref, b_ref, decay_ref, states, out_ref):
    ends = ends_of(accepted_ref)
    slot_owner = owner_of(ends, lax.broadcasted_iota(jnp.int32, (SLOTS, STATE), 0))
    x_all = x_ref[...]
    b_all = b_ref[...]
    for b in range(ROWS):
        mine = jnp.where(slot_owner == b, b_all, jnp.zeros((), bf16))
        added = lax.dot_general(x_all, mine, TN, preferred_element_type=f32)
        for h in range(4):
            at = slice(h * HEAD_DIM, (h + 1) * HEAD_DIM)
            scale = decay_ref[b : b + 1, h : h + 1]
            out_ref[b, at, :] = (states[b, at, :].astype(f32) * scale + added[at, :]).astype(bf16)


def tokens_kernel(idx_ref, *refs):
    pieces = refs[:8]
    w_merge, out_ref, hidden = refs[8:]
    fill_hidden(True, idx_ref[1], idx_ref[2], idx_ref[3], pieces, hidden)
    low = pl.multiple_of((idx_ref[0] & 1) * (WIDTH // 2), WIDTH // 2)
    out_ref[...] = jnp.dot(
        hidden[:, pl.ds(low, WIDTH // 2)], w_merge[...], preferred_element_type=f32
    )


def merge_kernel(idx_ref, *refs):
    pieces = refs[:8]
    gain_ref, w_low, w_high, part_a, part_b, out_ref, hidden = refs[8:]
    squares = fill_hidden(False, idx_ref[1], idx_ref[2], idx_ref[3], pieces, hidden)
    scale = lax.rsqrt(squares * (1.0 / WIDTH) + epsilon)
    half = WIDTH // 2
    total = part_a[...] + part_b[...]
    for i, w in enumerate((w_low, w_high)):
        at = slice(i * half, (i + 1) * half)
        rows = (hidden[:, at].astype(f32) * scale * gain_ref[:, at]).astype(bf16)
        total = total + jnp.dot(rows, w[...], preferred_element_type=f32)
    out_ref[...] = total.astype(bf16)


def gather_pairs(w_groups, y, z):
    row = jnp.arange(64, dtype=jnp.int32)
    block, half, kind, entry = row // 16, (row // 8) % 2, (row // 4) % 2, row % 4
    group = (y ^ block) * 2 + ((z // 2) ^ half)
    column = (entry * 2 + kind) * 8 + group
    order = (column[:, None] == jnp.arange(64, dtype=jnp.int32)[None, :]).astype(bf16)
    turned = lax.dot_general(order, w_groups, NT, preferred_element_type=f32).astype(bf16)
    blocks = [turned[:16]] + [over_y(turned[16 * d : 16 * d + 16], d) for d in (1, 2, 3)]
    mine = jnp.concatenate([block[:8] for block in blocks], axis=0)
    other = jnp.concatenate([block[8:] for block in blocks], axis=0)
    parts = [mine, over_z(mine, 1), over_z(other, 2), over_z(other, 3)]
    parts = parts + [over_core(part) for part in parts]
    return jnp.concatenate(parts, axis=0)


def pair_places(y, z, c):
    row = jnp.arange(256, dtype=jnp.int32)
    f, e, d = row // 128, (row // 32) % 4, (row // 8) % 4
    kind, entry = (row // 4) % 2, row % 4
    source = ((y ^ d) * 4 + (z ^ e)) * 2 + (c ^ f)
    column = kind * STATE + source * 4 + entry
    return (column[:, None] == jnp.arange(256, dtype=jnp.int32)[None, :]).astype(bf16)


def shape(dims, kind):
    return jax.ShapeDtypeStruct(dims, kind)


PARAMS = pltpu.CompilerParams(vmem_limit_bytes=40 * 1024 * 1024)


def on_device(
    token_ids,
    accepted,
    embedding,
    norm_gain,
    w_gate,
    w_input,
    w_groups,
    w_step,
    step_bias,
    decay_rate,
    skip_gain,
    w_output,
    states,
    draft_gain,
    w_merge,
):
    x = lax.axis_index("section")
    head = lax.axis_index("head")
    y, z, c = head // 8, (head // 2) % 4, head % 2
    place = jnp.stack([x, y, z, c]).astype(jnp.int32)
    vocab_local = embedding.shape[0]
    local_ids = token_ids.reshape(-1) - x * vocab_local
    inside = (local_ids >= 0) & (local_ids < vocab_local)
    looked = jnp.take(embedding, jnp.clip(local_ids, 0, vocab_local - 1), axis=0)
    looked = jnp.where(inside[:, None], looked, jnp.zeros((), bf16))
    found = [over_x(looked, s) for s in (1, 2, 3)]
    picked = pl.pallas_call(
        pick_kernel,
        out_shape=shape((SLOTS, CELL), bf16),
        in_specs=[SMEM] + [VMEM] * 4,
        out_specs=VMEM,
        name="pick",
    )(accepted, looked, *found)
    line = jnp.stack([picked] + [over_y(picked, d) for d in (1, 2, 3)])
    plane = [line] + [over_z(line, e) for e in (1, 2, 3)]
    embedded = plane + [over_core(part) for part in plane]

    w_pairs = gather_pairs(w_groups[0], y, z)
    pair_place = pair_places(y, z, c)
    step_rows = jnp.pad(w_step[0].T, ((0, 12), (0, 0)))
    start_states = states[0].reshape(ROWS, 4 * HEAD_DIM, STATE)
    w_high = route(w_merge, lambda x, y, z, c: (x - 1, y, z, c))

    kinds = (
        shape((4, SLOTS, CHUNK), f32),
        shape((4, SLOTS, CHUNK), bf16),
        shape((SLOTS, 4 * HEAD_DIM), bf16),
        shape((SLOTS, STATE), bf16),
        shape((16, 16), f32),
    )
    pieces = embedded
    saved = ()
    for tick in range(4):
        first = tick == 0
        kept, sent, *saved = pl.pallas_call(
            functools.partial(layer_kernel, first, tick),
            out_shape=kinds,
            in_specs=[SMEM] * 5 + [VMEM] * (16 + len(saved)),
            out_specs=(VMEM,) * 5,
            scratch_shapes=[pltpu.VMEM((SLOTS, WIDTH), bf16)] * 2,
            compiler_params=PARAMS,
            name="layer",
        )(
            accepted,
            place,
            step_bias,
            decay_rate,
            skip_gain,
            *pieces,
            norm_gain,
            w_gate[0],
            w_input[0],
            w_pairs,
            step_rows,
            w_output[0],
            start_states,
            pair_place,
            *saved,
        )
        if first:
            tokens_part = pl.pallas_call(
                tokens_kernel,
                out_shape=shape((SLOTS, CELL), f32),
                in_specs=[SMEM] + [VMEM] * 9,
                out_specs=VMEM,
                scratch_shapes=[pltpu.VMEM((SLOTS, WIDTH), bf16)],
                name="tokens",
            )(place, *embedded, w_merge)
            part_a = over_x(tokens_part, 2)
            part_b = over_x(tokens_part, 3)
        other = over_core(sent)
        summed = kept + other.astype(f32)
        across = [over_z(summed[e].astype(bf16), e) for e in (1, 2, 3)]
        total = summed[0]
        for part in across:
            total = total + part.astype(f32)
        total = total.astype(bf16)
        arrived = [next_section(total, d) for d in range(4)]
        own = arrived[0].astype(f32)
        for part in arrived[1:]:
            own = own + part.astype(f32)
        own = own.astype(bf16)
        pieces = [own] + [over_z(own, e) for e in (1, 2, 3)]
        pieces = pieces + [over_core(part) for part in pieces]

    kept_states = pl.pallas_call(
        state_kernel,
        out_shape=shape((ROWS, 4 * HEAD_DIM, STATE), bf16),
        in_specs=[SMEM] + [VMEM] * 4,
        out_specs=VMEM,
        name="kept",
    )(accepted, *saved, start_states)

    merged = pl.pallas_call(
        merge_kernel,
        out_shape=shape((SLOTS, CELL), bf16),
        in_specs=[SMEM] + [VMEM] * 13,
        out_specs=VMEM,
        scratch_shapes=[pltpu.VMEM((SLOTS, WIDTH), bf16)],
        name="merge",
    )(place, *pieces, draft_gain.reshape(1, WIDTH), w_merge, w_high, part_a, part_b)
    share = PACKED // 4
    draft = merged[:share]
    for s in (1, 2, 3):
        got = over_x(merged[share * s : share * (s + 1)], s)
        draft = jnp.where(x == s, got, draft)
    return (kept_states.reshape(1, ROWS, 4, HEAD_DIM, STATE), draft)


def solution(mesh):
    return jax.shard_map(
        on_device,
        mesh=mesh,
        in_specs=(
            P(),
            P(),
            P("section", "head"),
            P("section", None),
            P("section", None, "head"),
            P("section", None, "head"),
            P("section", None, "head"),
            P("section", None, "head"),
            P("section", "head"),
            P("section", "head"),
            P("section", "head"),
            P("section", "head", None),
            P("section", None, "head", None, None),
            P(),
            P("section", "head"),
        ),
        out_specs=(P("section", None, "head", None, None), P("section", "head")),
        check_vma=False,
    )
```

```python
import functools

import jax
import jax.numpy as jnp
from jax import lax
from jax.experimental import pallas as pl
from jax.experimental.pallas import tpu as pltpu
from jax.sharding import PartitionSpec as P

HEAD_DIM = 64
STATE = 128
GROUPS = 8
ACCEPTED = 36
POS = 5
ROWS = 12
PACKED = 2 * ACCEPTED
SLOTS = 80
WIDTH = 4096
CHUNK = 512
CELL = 128
SHARE = 24

epsilon = 1e-05
bf16 = jnp.bfloat16
f32 = jnp.float32

VMEM = pl.BlockSpec(memory_space=pltpu.VMEM)
SMEM = pl.BlockSpec(memory_space=pltpu.SMEM)
NT = (((1,), (1,)), ((), ()))
TN = (((0,), (0,)), ((), ()))


def route(value, target):
    pairs = []
    for source in range(128):
        goal = target(source >> 5, (source >> 3) & 3, (source >> 1) & 3, source & 1)
        if goal is not None:
            x, y, z, c = goal
            pairs.append((source, ((x & 3) << 5) | (y << 3) | (z << 1) | c))
    return lax.ppermute(value, ("section", "head"), pairs)


def over_core(value):
    return route(value, lambda x, y, z, c: (x, y, z, c ^ 1))


def over_z(value, e):
    return route(value, lambda x, y, z, c: (x, y, z ^ e, c))


def over_y(value, d):
    return route(value, lambda x, y, z, c: (x, y ^ d, z, c))


def over_x(value, s):
    return route(value, lambda x, y, z, c: (x ^ s, y, z, c))


def next_section(value, d):
    return route(value, lambda x, y, z, c: (x + 1, y ^ d, z, c))


def coordinates():
    head = lax.axis_index("head")
    return lax.axis_index("section"), head >> 3, (head >> 1) & 3, head & 1


def ends_of(accepted_ref):
    ends = []
    for r in range(2):
        total = 0
        row = []
        for b in range(ROWS):
            total = total + accepted_ref[r, b]
            row.append(total)
        ends.append(row)
    return ends


def owner_of(ends, slot):
    later = slot >= ACCEPTED
    inner = jnp.where(later, slot - ACCEPTED, slot)
    owner = jnp.zeros_like(slot)
    for b in range(ROWS):
        end = jnp.where(later, ends[1][b], ends[0][b])
        owner = owner + (inner >= end).astype(jnp.int32)
    return owner


def look_kernel(accepted_ref, tokens_ref, table_ref, out_ref, listed, held, sem):
    ends = ends_of(accepted_ref)
    vocab_local = table_ref.shape[0]
    base = lax.axis_index("section") * vocab_local
    for r in range(2):
        for b in range(ROWS):
            start = ends[r][b] - accepted_ref[r, b] + r * ACCEPTED
            for k in range(POS):
                listed[start + k] = tokens_ref[r, b, k]
    lane = lax.broadcasted_iota(jnp.int32, (1, CELL), 1)
    slot = lax.broadcasted_iota(jnp.int32, (SLOTS, CELL), 0)
    codes = []
    for g in range(PACKED // 8):
        code = jnp.full((1, CELL), -1, jnp.int32)
        for i in range(8):
            n = 8 * g + i
            local = listed[n] - base
            row = jnp.clip(local, 0, vocab_local - 1)
            block = pl.multiple_of((row >> 4) << 4, 16)
            pltpu.make_async_copy(
                table_ref.at[pl.ds(block, 16), :], held.at[pl.ds(16 * n, 16), :], sem
            ).start()
            code = jnp.where(lane == 16 * i + (row & 15), jnp.where(local == row, n, -1), code)
        codes.append(code)
    picks = [(slot == code).astype(bf16) for code in codes]
    pltpu.make_async_copy(table_ref.at[pl.ds(0, held.shape[0]), :], held, sem).wait()
    total = jnp.zeros((SLOTS, CELL), f32)
    for g, pick in enumerate(picks):
        total = total + jnp.dot(
            pick, held[g * CELL : (g + 1) * CELL, :], preferred_element_type=f32
        )
    out_ref[...] = total.astype(bf16)


def softplus(v):
    return jnp.maximum(v, 0.0) + jnp.log1p(jnp.exp(-jnp.abs(v)))


def fill_hidden(first, y, z, c, pieces, hidden):
    total = jnp.zeros((SLOTS, CELL), f32)
    for f in range(2):
        for e in range(4):
            if first:
                for d in range(4):
                    place = ((y ^ d) * 4 + (z ^ e)) * 2 + (c ^ f)
                    part = pieces[f][e, d]
                    hidden[:, pl.ds(pl.multiple_of(place * CELL, CELL), CELL)] = part
                    wide = part.astype(f32)
                    total = total + wide * wide
            else:
                place = (c ^ f) * 4 + (z ^ e)
                part = pieces[f][e]
                hidden[:, pl.ds(pl.multiple_of(place * CHUNK, CHUNK), CHUNK)] = part
                wide = part.astype(f32)
                square = wide * wide
                for i in range(CHUNK // CELL):
                    total = total + square[:, i * CELL : (i + 1) * CELL]
    return jnp.sum(total, axis=1, keepdims=True)


def share_rows(section):
    row = lax.broadcasted_iota(jnp.int32, (SHARE, SLOTS), 0)
    slot = lax.broadcasted_iota(jnp.int32, (SHARE, SLOTS), 1)
    return ((row < PACKED // 4) & (slot == section * (PACKED // 4) + row)).astype(bf16)


def project(last, gated, w_output, side, z, out_ref):
    for e in range(4):
        place = side * 4 + (e if last else z ^ e)
        w = w_output[:, pl.ds(pl.multiple_of(place * CHUNK, CHUNK), CHUNK)]
        part = jnp.dot(gated, w, preferred_element_type=f32).astype(out_ref.dtype)
        if last:
            for g in range(4):
                out_ref[g, :, e * CHUNK : (e + 1) * CHUNK] = part[g * SHARE : (g + 1) * SHARE]
        else:
            out_ref[e] = part


def keep_kernel(last, gated_ref, own_ref, w_output, out_ref):
    _, _, z, c = coordinates()
    project(last, gated_ref[...], w_output, c, z, out_ref)
    out_ref[0] += own_ref[...].astype(f32)


def layer_kernel(first, last, tick, *refs):
    (accepted_ref, bias_ref, rate_ref, skip_ref) = refs[:4]
    pieces = refs[4:6]
    (gain_ref, w_gate, w_input, w_pairs, w_step, w_output, states, place_ref) = refs[6:14]
    refs = refs[14:]
    if not first:
        old_x, old_b, old_decay = refs[:3]
        refs = refs[3:]
    gated_ref, own_ref, sent_ref, new_x, new_b, new_decay = refs[:6]
    hidden, normed = refs[-2:]
    x, y, z, c = coordinates()
    ends = ends_of(accepted_ref)

    squares = fill_hidden(first, y, z, c, pieces, hidden)
    scale = lax.rsqrt(squares * (1.0 / WIDTH) + epsilon)
    for i in range(WIDTH // CHUNK):
        at = slice(i * CHUNK, (i + 1) * CHUNK)
        normed[:, at] = (hidden[:, at].astype(f32) * scale * gain_ref[:, at]).astype(bf16)
    rows = normed[...]
    gate = jnp.dot(rows, w_gate[...], preferred_element_type=f32)
    inner = jnp.dot(rows, w_input[...], preferred_element_type=f32)
    pairs = lax.dot_general(rows, w_pairs[...], NT, preferred_element_type=f32).astype(bf16)
    pairs = jnp.dot(pairs, place_ref[...], preferred_element_type=f32).astype(bf16)
    b_vec, c_vec = pairs[:, :STATE], pairs[:, STATE:]
    raw = lax.dot_general(rows, w_step[...], NT, preferred_element_type=f32)

    lane = lax.broadcasted_iota(jnp.int32, (1, 16), 1)
    bias = jnp.zeros((1, 16), f32)
    rate = jnp.zeros((1, 16), f32)
    for h in range(4):
        bias = jnp.where(lane == h, bias_ref[0, h], bias)
        rate = jnp.where(lane == h, rate_ref[0, h], rate)
    step = softplus(raw + bias)
    fall = step * rate

    row_owner = owner_of(ends, lax.broadcasted_iota(jnp.int32, (SLOTS, SLOTS), 0))
    col_owner = owner_of(ends, lax.broadcasted_iota(jnp.int32, (SLOTS, SLOTS), 1))
    same = row_owner == col_owner
    ahead = lax.broadcasted_iota(jnp.int32, (SLOTS, SLOTS), 1) <= lax.broadcasted_iota(
        jnp.int32, (SLOTS, SLOTS), 0
    )
    causal = same & ahead
    causal_f32 = causal.astype(f32)
    log_decay = -jnp.dot(
        causal_f32, fall, precision=lax.Precision.HIGHEST, preferred_element_type=f32
    )
    log_decay_t = -lax.dot_general(
        fall,
        causal_f32,
        (((0,), (1,)), ((), ())),
        precision=lax.Precision.HIGHEST,
        preferred_element_type=f32,
    )
    after = (same & jnp.logical_not(ahead)).astype(f32)
    rest = -jnp.dot(after, fall, precision=lax.Precision.HIGHEST, preferred_element_type=f32)
    batch = lax.broadcasted_iota(jnp.int32, (16, SLOTS), 0)
    batch_owner = owner_of(ends, lax.broadcasted_iota(jnp.int32, (16, SLOTS), 1))
    total = -jnp.dot(
        (batch == batch_owner).astype(f32),
        fall,
        precision=lax.Precision.HIGHEST,
        preferred_element_type=f32,
    )

    products = lax.dot_general(c_vec, b_vec, NT, preferred_element_type=f32)
    slot_owner = owner_of(ends, lax.broadcasted_iota(jnp.int32, (SLOTS, STATE), 0))
    carried = jnp.zeros((SLOTS, 4 * HEAD_DIM), f32)
    for b in range(ROWS):
        mine = jnp.where(slot_owner == b, c_vec, jnp.zeros((), bf16))
        carried = carried + lax.dot_general(mine, states[b], NT, preferred_element_type=f32)

    wide_lane = lax.broadcasted_iota(jnp.int32, (SLOTS, 2 * HEAD_DIM), 1)
    left = wide_lane < HEAD_DIM

    def spread(v, p):
        return jnp.where(left, v[:, 2 * p : 2 * p + 1], v[:, 2 * p + 1 : 2 * p + 2])

    gated = []
    weighted = []
    for p in range(2):
        at = slice(p * 128, (p + 1) * 128)
        x_p = inner[:, at]
        dx = spread(step, p) * x_p
        dx_b = dx.astype(bf16)
        mixed = []
        for h in (2 * p, 2 * p + 1):
            gap = log_decay[:, h : h + 1] - log_decay_t[h : h + 1, :]
            weights = products * jnp.exp(jnp.where(causal, gap, -1e30))
            mixed.append(jnp.dot(weights.astype(bf16), dx_b, preferred_element_type=f32))
        out = jnp.where(left, mixed[0], mixed[1])
        out = out + jnp.exp(spread(log_decay, p)) * carried[:, at]
        skip = jnp.where(left, skip_ref[0, 2 * p], skip_ref[0, 2 * p + 1])
        out = out + skip * x_p
        g = gate[:, at]
        gated.append((out * (g / (1.0 + jnp.exp(-g)))).astype(bf16))
        weighted.append((jnp.exp(spread(rest, p)) * dx).astype(bf16))
    gated = jnp.concatenate(gated, axis=1)

    half = WIDTH // 2
    if last:
        order = jnp.concatenate([share_rows(z ^ e) for e in range(4)], axis=0)
        gated = jnp.dot(order, gated, preferred_element_type=f32).astype(bf16)
        own = hidden[:, pl.ds(pl.multiple_of(c * half, half), half)]
        own = jnp.dot(order[:SHARE], own, preferred_element_type=f32).astype(bf16)
    else:
        place = c * 4 + z
        own = hidden[:, pl.ds(pl.multiple_of(place * CHUNK, CHUNK), CHUNK)]
    gated_ref[...] = gated
    own_ref[...] = jnp.where(y == 0, own, jnp.zeros((), bf16))
    project(last, gated, w_output, c ^ 1, z, sent_ref)

    decay = jnp.exp(total)
    if first:
        share = share_rows(x)
        refs[6][...] = jnp.dot(share, hidden[...], preferred_element_type=f32).astype(bf16)
        new_x[:, :128] = weighted[0]
        new_x[:, 128:] = weighted[1]
        new_b[...] = b_vec
        new_decay[...] = decay
    else:
        now = x == tick
        new_x[:, :128] = jnp.where(now, weighted[0], old_x[:, :128])
        new_x[:, 128:] = jnp.where(now, weighted[1], old_x[:, 128:])
        new_b[...] = jnp.where(now, b_vec, old_b[...])
        new_decay[...] = jnp.where(now, decay, old_decay[...])


def state_kernel(accepted_ref, x_ref, b_ref, decay_ref, states, out_ref):
    ends = ends_of(accepted_ref)
    slot_owner = owner_of(ends, lax.broadcasted_iota(jnp.int32, (SLOTS, STATE), 0))
    x_all = x_ref[...]
    b_all = b_ref[...]
    for b in range(ROWS):
        mine = jnp.where(slot_owner == b, b_all, jnp.zeros((), bf16))
        added = lax.dot_general(x_all, mine, TN, preferred_element_type=f32)
        for h in range(4):
            at = slice(h * HEAD_DIM, (h + 1) * HEAD_DIM)
            scale = decay_ref[b : b + 1, h : h + 1]
            out_ref[b, at, :] = (states[b, at, :].astype(f32) * scale + added[at, :]).astype(bf16)


def add_products(x, rows, weights, low, total):
    half = WIDTH // 2
    w_own, w_far, w_pair = weights
    for way, w in ((0, w_own), (3, w_far), (1, w_pair.at[0]), (2, w_pair.at[1])):
        block = x ^ way

        @pl.when((block >= low) & (block < low + 2))
        def _():
            at = pl.ds(pl.multiple_of((block - low) * half, half), half)
            total[...] += jnp.dot(rows[:, at], w[...], preferred_element_type=f32)


def tokens_kernel(tokens_ref, *refs):
    out_ref = refs[3]
    out_ref[...] = jnp.zeros((SHARE, CELL), f32)
    add_products(lax.axis_index("section"), tokens_ref, refs[:3], 2, out_ref)


def merge_kernel(own_ref, other_ref, part_ref, gain_ref, *refs):
    out_ref, joined, total = refs[3:]
    x, _, _, c = coordinates()
    half = WIDTH // 2
    squares = jnp.zeros((SHARE, 1), f32)
    for ref in (own_ref, other_ref):
        wide = ref[...].astype(f32)
        squares = squares + jnp.sum(wide * wide, axis=1, keepdims=True)
    scale = lax.rsqrt(squares * (1.0 / WIDTH) + epsilon)
    for f, ref in enumerate((own_ref, other_ref)):
        at = pl.ds(pl.multiple_of((c ^ f) * half, half), half)
        joined[:, at] = (ref[...].astype(f32) * scale * gain_ref[:, at]).astype(bf16)
    total[...] = part_ref[...]
    add_products(x, joined, refs[:3], 0, total)
    out_ref[...] = total[: PACKED // 4, :].astype(bf16)


def turn_groups(w_groups, y, z):
    row = jnp.arange(64, dtype=jnp.int32)
    block, half, kind, entry = row // 16, (row // 8) % 2, (row // 4) % 2, row % 4
    group = (y ^ block) * 2 + ((z // 2) ^ half)
    column = (entry * 2 + kind) * 8 + group
    order = (column[:, None] == jnp.arange(64, dtype=jnp.int32)[None, :]).astype(bf16)
    return lax.dot_general(order, w_groups, NT, preferred_element_type=f32).astype(bf16)


def pair_places(y, z, c):
    row = jnp.arange(256, dtype=jnp.int32)
    f, e, d = row // 128, (row // 32) % 4, (row // 8) % 4
    kind, entry = (row // 4) % 2, row % 4
    source = ((y ^ d) * 4 + (z ^ e)) * 2 + (c ^ f)
    column = kind * STATE + source * 4 + entry
    return (column[:, None] == jnp.arange(256, dtype=jnp.int32)[None, :]).astype(bf16)


def shape(dims, kind):
    return jax.ShapeDtypeStruct(dims, kind)


PARAMS = pltpu.CompilerParams(vmem_limit_bytes=40 * 1024 * 1024)
KEEP_BYTES = 8 * 10**6
SMALL = pltpu.CompilerParams(vmem_limit_bytes=8 * 1024 * 1024)


def on_device(
    token_ids,
    accepted,
    embedding,
    norm_gain,
    w_gate,
    w_input,
    w_groups,
    w_step,
    step_bias,
    decay_rate,
    skip_gain,
    w_output,
    states,
    draft_gain,
    w_merge,
):
    x = lax.axis_index("section")
    head = lax.axis_index("head")
    y, z, c = head // 8, (head // 2) % 4, head % 2
    turned = turn_groups(w_groups[0], y, z)
    blocks = [turned[:16]] + [over_y(turned[16 * d : 16 * d + 16], d) for d in (1, 2, 3)]
    looked = pl.pallas_call(
        look_kernel,
        out_shape=shape((SLOTS, CELL), bf16),
        in_specs=[SMEM] * 2 + [pl.BlockSpec(memory_space=pl.ANY)],
        out_specs=VMEM,
        scratch_shapes=[
            pltpu.SMEM((2 * ROWS * POS,), jnp.int32),
            pltpu.VMEM((16 * PACKED, CELL), bf16),
            pltpu.SemaphoreType.DMA,
        ],
        cost_estimate=pl.CostEstimate(flops=10**9, bytes_accessed=10**7, transcendentals=0),
        compiler_params=SMALL,
        name="look",
    )(accepted, token_ids, embedding)
    looked, blocks, w_far = lax.optimization_barrier((looked, blocks, over_x(w_merge, 3)))
    found = [over_x(looked, s) for s in (1, 3, 2)]
    picked = looked.astype(f32)
    for part in found:
        picked = picked + part.astype(f32)
    picked = picked.astype(bf16)
    mine = jnp.concatenate([block[:8] for block in blocks], axis=0)
    other = jnp.concatenate([block[8:] for block in blocks], axis=0)
    pairs_half = [mine, over_z(mine, 1), over_z(other, 2), over_z(other, 3)]
    line = jnp.stack([picked] + [over_y(picked, d) for d in (1, 2, 3)])
    line, pairs_half = lax.optimization_barrier((line, pairs_half))
    pairs_half = jnp.concatenate(pairs_half, axis=0)
    w_pairs = jnp.concatenate([pairs_half, over_core(pairs_half)], axis=0)
    plane = jnp.stack([line] + [over_z(line, e) for e in (1, 2, 3)])

    pair_place = pair_places(y, z, c)
    step_rows = jnp.pad(w_step[0].T, ((0, 12), (0, 0)))
    start_states = states[0].reshape(ROWS, 4 * HEAD_DIM, STATE)
    pieces = (plane, over_core(plane))
    w_pair = jnp.stack([w_merge, w_far])

    saved_kinds = (
        shape((SLOTS, 4 * HEAD_DIM), bf16),
        shape((SLOTS, STATE), bf16),
        shape((16, 16), f32),
    )
    saved = ()
    for tick in range(4):
        first, last = tick == 0, tick == 3
        part = (4, SHARE, WIDTH // 2) if last else (4, SLOTS, CHUNK)
        kinds = (
            shape((4 * SHARE if last else SLOTS, 4 * HEAD_DIM), bf16),
            shape(part[1:], bf16),
            shape(part, bf16),
        ) + saved_kinds
        if first:
            kinds = kinds + (shape((SHARE, WIDTH), bf16),)
        gated, own, sent, *saved = pl.pallas_call(
            functools.partial(layer_kernel, first, last, tick),
            out_shape=kinds,
            in_specs=[SMEM] * 4 + [VMEM] * (10 + len(saved)),
            out_specs=(VMEM,) * len(kinds),
            scratch_shapes=[pltpu.VMEM((SLOTS, WIDTH), bf16)] * 2,
            compiler_params=PARAMS,
            name="layer",
        )(
            accepted,
            step_bias,
            decay_rate,
            skip_gain,
            *pieces,
            norm_gain,
            w_gate[0],
            w_input[0],
            w_pairs,
            step_rows,
            w_output[0],
            start_states,
            pair_place,
            *saved,
        )
        if first:
            tokens = saved.pop()
        kept = pl.pallas_call(
            functools.partial(keep_kernel, last),
            out_shape=shape(part, f32),
            in_specs=[VMEM] * 3,
            out_specs=VMEM,
            compiler_params=SMALL,
            cost_estimate=pl.CostEstimate(
                flops=10**8, bytes_accessed=KEEP_BYTES, transcendentals=0
            ),
            name="keep",
        )(gated, own, w_output[0])
        other = over_core(sent)
        if last:
            other, w_pair = lax.optimization_barrier((other, w_pair))
        summed = kept + other.astype(f32)
        across = [over_z(summed[e].astype(bf16), e) for e in (1, 2, 3)]
        total = summed[0]
        for part in across:
            total = total + part.astype(f32)
        total = total.astype(bf16)
        if last:
            break
        arrived = [next_section(total, d) for d in range(4)]
        own = arrived[0].astype(f32)
        for part in arrived[1:]:
            own = own + part.astype(f32)
        own = own.astype(bf16)
        if tick == 2:
            own, w_pair = lax.optimization_barrier((own, w_pair))
            w_pair = over_x(w_pair, 1)
        plane = jnp.stack([own] + [over_z(own, e) for e in (1, 2, 3)])
        pieces = (plane, over_core(plane))

    kept_states = pl.pallas_call(
        state_kernel,
        out_shape=shape((ROWS, 4 * HEAD_DIM, STATE), bf16),
        in_specs=[SMEM] + [VMEM] * 4,
        out_specs=VMEM,
        compiler_params=SMALL,
        name="kept",
    )(accepted, *saved, start_states)

    tokens_part = pl.pallas_call(
        tokens_kernel,
        out_shape=shape((SHARE, CELL), f32),
        in_specs=[VMEM] * 4,
        out_specs=VMEM,
        compiler_params=SMALL,
        name="tokens",
    )(tokens, w_merge, w_far, w_pair)
    parts = [over_y(total, d) for d in (1, 2, 3)]
    parts, kept_states, tokens_part = lax.optimization_barrier((parts, kept_states, tokens_part))
    final = total.astype(f32)
    for part in parts:
        final = final + part.astype(f32)
    final = final.astype(bf16)
    rows = [
        route(final, lambda x, y, z, c, k=k: (z, y, z ^ k, c) if x == 3 else None)
        for k in range(4)
    ]
    rows = (rows[0] + rows[1]) + (rows[2] + rows[3])
    draft = pl.pallas_call(
        merge_kernel,
        out_shape=shape((PACKED // 4, CELL), bf16),
        in_specs=[VMEM] * 7,
        out_specs=VMEM,
        scratch_shapes=[pltpu.VMEM((SHARE, WIDTH), bf16), pltpu.VMEM((SHARE, CELL), f32)],
        compiler_params=SMALL,
        name="merge",
    )(rows, over_core(rows), tokens_part, draft_gain.reshape(1, WIDTH), w_merge, w_far, w_pair)
    return (kept_states.reshape(1, ROWS, 4, HEAD_DIM, STATE), draft)


def solution(mesh):
    return jax.shard_map(
        on_device,
        mesh=mesh,
        in_specs=(
            P(),
            P(),
            P("section", "head"),
            P("section", None),
            P("section", None, "head"),
            P("section", None, "head"),
            P("section", None, "head"),
            P("section", None, "head"),
            P("section", "head"),
            P("section", "head"),
            P("section", "head"),
            P("section", "head", None),
            P("section", None, "head", None, None),
            P(),
            P("section", "head"),
        ),
        out_specs=(P("section", None, "head", None, None), P("section", "head")),
        check_vma=False,
    )
```

```python
import functools

import jax
import jax.numpy as jnp
from jax import lax
from jax.experimental import pallas as pl
from jax.experimental.pallas import tpu as pltpu
from jax.sharding import PartitionSpec as P

HEAD_DIM = 64
STATE = 128
GROUPS = 8
ACCEPTED = 36
POS = 5
ROWS = 12
PACKED = 2 * ACCEPTED
SLOTS = 80
WIDTH = 4096
CHUNK = 512
CELL = 128
SHARE = 24

epsilon = 1e-05
bf16 = jnp.bfloat16
f32 = jnp.float32

VMEM = pl.BlockSpec(memory_space=pltpu.VMEM)
SMEM = pl.BlockSpec(memory_space=pltpu.SMEM)
NT = (((1,), (1,)), ((), ()))
TN = (((0,), (0,)), ((), ()))


def route(value, target):
    pairs = []
    for source in range(128):
        goal = target(source >> 5, (source >> 3) & 3, (source >> 1) & 3, source & 1)
        if goal is not None:
            x, y, z, c = goal
            pairs.append((source, ((x & 3) << 5) | (y << 3) | (z << 1) | c))
    return lax.ppermute(value, ("section", "head"), pairs)


def over_core(value):
    return route(value, lambda x, y, z, c: (x, y, z, c ^ 1))


def over_z(value, e):
    return route(value, lambda x, y, z, c: (x, y, z ^ e, c))


def over_y(value, d):
    return route(value, lambda x, y, z, c: (x, y ^ d, z, c))


def over_x(value, s):
    return route(value, lambda x, y, z, c: (x ^ s, y, z, c))


def next_section(value, d):
    return route(value, lambda x, y, z, c: (x + 1, y ^ d, z, c))


def coordinates():
    head = lax.axis_index("head")
    return lax.axis_index("section"), head >> 3, (head >> 1) & 3, head & 1


def ends_of(accepted_ref):
    ends = []
    for r in range(2):
        total = 0
        row = []
        for b in range(ROWS):
            total = total + accepted_ref[r, b]
            row.append(total)
        ends.append(row)
    return ends


def owner_of(ends, slot):
    later = slot >= ACCEPTED
    inner = jnp.where(later, slot - ACCEPTED, slot)
    owner = jnp.zeros_like(slot)
    for b in range(ROWS):
        end = jnp.where(later, ends[1][b], ends[0][b])
        owner = owner + (inner >= end).astype(jnp.int32)
    return owner


def look_kernel(accepted_ref, tokens_ref, table_ref, out_ref, listed, held, sem):
    ends = ends_of(accepted_ref)
    vocab_local = table_ref.shape[0]
    base = lax.axis_index("section") * vocab_local
    for r in range(2):
        for b in range(ROWS):
            start = ends[r][b] - accepted_ref[r, b] + r * ACCEPTED
            for k in range(POS):
                listed[start + k] = tokens_ref[r, b, k]
    lane = lax.broadcasted_iota(jnp.int32, (1, CELL), 1)
    slot = lax.broadcasted_iota(jnp.int32, (SLOTS, CELL), 0)
    codes = []
    for g in range(PACKED // 8):
        code = jnp.full((1, CELL), -1, jnp.int32)
        for i in range(8):
            n = 8 * g + i
            local = listed[n] - base
            row = jnp.clip(local, 0, vocab_local - 1)
            block = pl.multiple_of((row >> 4) << 4, 16)
            pltpu.make_async_copy(
                table_ref.at[pl.ds(block, 16), :], held.at[pl.ds(16 * n, 16), :], sem
            ).start()
            code = jnp.where(lane == 16 * i + (row & 15), jnp.where(local == row, n, -1), code)
        codes.append(code)
    picks = [(slot == code).astype(bf16) for code in codes]
    pltpu.make_async_copy(table_ref.at[pl.ds(0, held.shape[0]), :], held, sem).wait()
    total = jnp.zeros((SLOTS, CELL), f32)
    for g, pick in enumerate(picks):
        total = total + jnp.dot(
            pick, held[g * CELL : (g + 1) * CELL, :], preferred_element_type=f32
        )
    out_ref[...] = total.astype(bf16)


def softplus(v):
    return jnp.maximum(v, 0.0) + jnp.log1p(jnp.exp(-jnp.abs(v)))


def fill_rows(first, y, z, c, pieces, gain_ref, rows, hidden):
    total = jnp.zeros((SLOTS, CELL), f32)
    for f in range(2):
        for e in range(4):
            for d in range(4):
                if first:
                    place = ((y ^ d) * 4 + (z ^ e)) * 2 + (c ^ f)
                    part = pieces[f][e, d]
                else:
                    place = ((c ^ f) * 4 + (z ^ e)) * 4 + d
                    part = pieces[f][e, :, d * CELL : (d + 1) * CELL]
                at = pl.ds(pl.multiple_of(place * CELL, CELL), CELL)
                wide = part.astype(f32)
                total = total + wide * wide
                rows[:, at] = (wide * gain_ref[:, at]).astype(bf16)
                if first:
                    hidden[:, at] = part
    return jnp.sum(total, axis=1, keepdims=True)


def share_rows(section):
    row = lax.broadcasted_iota(jnp.int32, (SHARE, SLOTS), 0)
    slot = lax.broadcasted_iota(jnp.int32, (SHARE, SLOTS), 1)
    return ((row < PACKED // 4) & (slot == section * (PACKED // 4) + row)).astype(bf16)


def plan_kernel(accepted_ref, causal_ref, after_ref, batch_ref, owner_ref):
    ends = ends_of(accepted_ref)
    slots = (SLOTS, SLOTS)
    row = lax.broadcasted_iota(jnp.int32, slots, 0)
    column = lax.broadcasted_iota(jnp.int32, slots, 1)
    same = owner_of(ends, row) == owner_of(ends, column)
    causal_ref[...] = (same & (column <= row)).astype(f32)
    after_ref[...] = (same & (column > row)).astype(f32)
    batch = lax.broadcasted_iota(jnp.int32, (16, SLOTS), 0)
    batch_owner = owner_of(ends, lax.broadcasted_iota(jnp.int32, (16, SLOTS), 1))
    batch_ref[...] = (batch == batch_owner).astype(f32)
    owner_ref[...] = owner_of(ends, lax.broadcasted_iota(jnp.int32, (SLOTS, STATE), 0))


def project(last, gated, w_output, side, z, out_ref):
    for e in range(4):
        place = side * 4 + (e if last else z ^ e)
        w = w_output[:, pl.ds(pl.multiple_of(place * CHUNK, CHUNK), CHUNK)]
        part = jnp.dot(gated, w, preferred_element_type=f32).astype(out_ref.dtype)
        if last:
            for g in range(4):
                out_ref[g, :, e * CHUNK : (e + 1) * CHUNK] = part[g * SHARE : (g + 1) * SHARE]
        else:
            out_ref[e] = part


def keep_kernel(last, gated_ref, own_ref, w_output, out_ref):
    _, _, z, c = coordinates()
    project(last, gated_ref[...], w_output, c, z, out_ref)
    out_ref[0] += own_ref[...].astype(f32)


def layer_kernel(first, last, tick, *refs):
    (bias_ref, rate_ref, skip_ref) = refs[:3]
    (causal_ref, after_ref, batch_ref, owner_ref) = refs[3:7]
    pieces = refs[7:9]
    (gain_ref, w_gate, w_input, w_pairs, w_step, w_output, states) = refs[9:16]
    refs = refs[16:]
    if first:
        place_ref = refs[0]
        refs = refs[1:]
    if not first:
        old_x, old_b, old_decay = refs[:3]
        refs = refs[3:]
    gated_ref, own_ref, sent_ref, new_x, new_b, new_decay = refs[:6]
    if first:
        hidden = refs[-2]
    else:
        hidden = None
    filled = refs[-1]
    x, y, z, c = coordinates()

    squares = fill_rows(first, y, z, c, pieces, gain_ref, filled, hidden)
    scale = lax.rsqrt(squares * (1.0 / WIDTH) + epsilon)
    rows = filled[...]
    if first:
        pairs = lax.dot_general(rows, w_pairs[...], NT, preferred_element_type=f32) * scale
        pairs = jnp.dot(pairs.astype(bf16), place_ref[...], preferred_element_type=f32)
    else:
        pairs = jnp.dot(rows, w_pairs[...], preferred_element_type=f32) * scale
    pairs = pairs.astype(bf16)
    b_vec, c_vec = pairs[:, :STATE], pairs[:, STATE:]
    raw = jnp.dot(rows, w_step[...], preferred_element_type=f32) * scale
    inner = jnp.dot(rows, w_input[...], preferred_element_type=f32) * scale
    gate = jnp.dot(rows, w_gate[...], preferred_element_type=f32) * scale

    lane = lax.broadcasted_iota(jnp.int32, (1, CELL), 1)
    bias = jnp.zeros((1, CELL), f32)
    rate = jnp.zeros((1, CELL), f32)
    for h in range(4):
        bias = jnp.where(lane == h, bias_ref[0, h], bias)
        rate = jnp.where(lane == h, rate_ref[0, h], rate)
    step = softplus(raw + bias)
    fall = step * rate

    causal_f32 = causal_ref[...]
    causal = causal_f32 > 0.0
    log_decay = -jnp.dot(
        causal_f32, fall, precision=lax.Precision.HIGHEST, preferred_element_type=f32
    )
    log_decay_t = -lax.dot_general(
        fall,
        causal_f32,
        (((0,), (1,)), ((), ())),
        precision=lax.Precision.HIGHEST,
        preferred_element_type=f32,
    )
    rest = -jnp.dot(
        after_ref[...], fall, precision=lax.Precision.HIGHEST, preferred_element_type=f32
    )
    total = -jnp.dot(
        batch_ref[...], fall, precision=lax.Precision.HIGHEST, preferred_element_type=f32
    )

    products = lax.dot_general(c_vec, b_vec, NT, preferred_element_type=f32)
    slot_owner = owner_ref[...]
    carried = jnp.zeros((SLOTS, 4 * HEAD_DIM), f32)
    for b in range(ROWS):
        mine = jnp.where(slot_owner == b, c_vec, jnp.zeros((), bf16))
        carried = carried + lax.dot_general(mine, states[b], NT, preferred_element_type=f32)

    wide_lane = lax.broadcasted_iota(jnp.int32, (SLOTS, 2 * HEAD_DIM), 1)
    left = wide_lane < HEAD_DIM

    def spread(v, p):
        return jnp.where(left, v[:, 2 * p : 2 * p + 1], v[:, 2 * p + 1 : 2 * p + 2])

    gated = []
    weighted = []
    for p in range(2):
        at = slice(p * 128, (p + 1) * 128)
        x_p = inner[:, at]
        dx = spread(step, p) * x_p
        dx_b = dx.astype(bf16)
        mixed = []
        for h in (2 * p, 2 * p + 1):
            gap = log_decay[:, h : h + 1] - log_decay_t[h : h + 1, :]
            weights = products * jnp.exp(jnp.where(causal, gap, -1e30))
            mixed.append(jnp.dot(weights.astype(bf16), dx_b, preferred_element_type=f32))
        out = jnp.where(left, mixed[0], mixed[1])
        out = out + jnp.exp(spread(log_decay, p)) * carried[:, at]
        skip = jnp.where(left, skip_ref[0, 2 * p], skip_ref[0, 2 * p + 1])
        out = out + skip * x_p
        g = gate[:, at]
        gated.append((out * (g / (1.0 + jnp.exp(-g)))).astype(bf16))
        weighted.append((jnp.exp(spread(rest, p)) * dx).astype(bf16))
    gated = jnp.concatenate(gated, axis=1)

    if last:
        order = jnp.concatenate([share_rows(z ^ e) for e in range(4)], axis=0)
        gated = jnp.dot(order, gated, preferred_element_type=f32).astype(bf16)
        for k in range(4):
            own = jnp.dot(order[:SHARE], pieces[0][z ^ k], preferred_element_type=f32)
            own_ref[:, k * CHUNK : (k + 1) * CHUNK] = jnp.where(y == 0, own, 0.0).astype(bf16)
    else:
        if first:
            place = c * 4 + z
            own = hidden[:, pl.ds(pl.multiple_of(place * CHUNK, CHUNK), CHUNK)]
        else:
            own = pieces[0][0]
        own_ref[...] = jnp.where(y == 0, own, jnp.zeros((), bf16))
    gated_ref[...] = gated
    project(last, gated, w_output, c ^ 1, z, sent_ref)

    decay = jnp.exp(total)
    if first:
        share = share_rows(x)
        refs[6][...] = jnp.dot(share, hidden[...], preferred_element_type=f32).astype(bf16)
        new_x[:, :128] = weighted[0]
        new_x[:, 128:] = weighted[1]
        new_b[...] = b_vec
        new_decay[...] = decay
    else:
        now = x == tick
        new_x[:, :128] = jnp.where(now, weighted[0], old_x[:, :128])
        new_x[:, 128:] = jnp.where(now, weighted[1], old_x[:, 128:])
        new_b[...] = jnp.where(now, b_vec, old_b[...])
        new_decay[...] = jnp.where(now, decay, old_decay[...])


def state_kernel(owner_ref, x_ref, b_ref, decay_ref, states, out_ref):
    slot_owner = owner_ref[...]
    x_all = x_ref[...]
    b_all = b_ref[...]
    for b in range(ROWS):
        mine = jnp.where(slot_owner == b, b_all, jnp.zeros((), bf16))
        added = lax.dot_general(x_all, mine, TN, preferred_element_type=f32)
        for h in range(4):
            at = slice(h * HEAD_DIM, (h + 1) * HEAD_DIM)
            scale = decay_ref[b : b + 1, h : h + 1]
            out_ref[b, at, :] = (states[b, at, :].astype(f32) * scale + added[at, :]).astype(bf16)


def add_products(x, rows, weights, low, total):
    half = WIDTH // 2
    w_own, w_far, w_pair = weights
    for way, w in ((0, w_own), (3, w_far), (1, w_pair.at[0]), (2, w_pair.at[1])):
        block = x ^ way

        @pl.when((block >= low) & (block < low + 2))
        def _():
            at = pl.ds(pl.multiple_of((block - low) * half, half), half)
            total[...] += jnp.dot(rows[:, at], w[...], preferred_element_type=f32)


def tokens_kernel(tokens_ref, *refs):
    out_ref = refs[3]
    out_ref[...] = jnp.zeros((SHARE, CELL), f32)
    add_products(lax.axis_index("section"), tokens_ref, refs[:3], 2, out_ref)


def merge_kernel(own_ref, other_ref, part_ref, gain_ref, *refs):
    out_ref, joined, total = refs[3:]
    x, _, _, c = coordinates()
    half = WIDTH // 2
    squares = jnp.zeros((SHARE, 1), f32)
    for ref in (own_ref, other_ref):
        wide = ref[...].astype(f32)
        squares = squares + jnp.sum(wide * wide, axis=1, keepdims=True)
    scale = lax.rsqrt(squares * (1.0 / WIDTH) + epsilon)
    for f, ref in enumerate((own_ref, other_ref)):
        at = pl.ds(pl.multiple_of((c ^ f) * half, half), half)
        joined[:, at] = (ref[...].astype(f32) * scale * gain_ref[:, at]).astype(bf16)
    total[...] = part_ref[...]
    add_products(x, joined, refs[:3], 0, total)
    out_ref[...] = total[: PACKED // 4, :].astype(bf16)


def turn_groups(w_groups, y, z):
    row = jnp.arange(64, dtype=jnp.int32)
    block, half, kind, entry = row // 16, (row // 8) % 2, (row // 4) % 2, row % 4
    group = (y ^ block) * 2 + ((z // 2) ^ half)
    column = (entry * 2 + kind) * 8 + group
    order = (column[:, None] == jnp.arange(64, dtype=jnp.int32)[None, :]).astype(bf16)
    return lax.dot_general(order, w_groups, NT, preferred_element_type=f32).astype(bf16)


def pair_places(y, z, c):
    row = jnp.arange(256, dtype=jnp.int32)
    f, e, d = row // 128, (row // 32) % 4, (row // 8) % 4
    kind, entry = (row // 4) % 2, row % 4
    source = ((y ^ d) * 4 + (z ^ e)) * 2 + (c ^ f)
    column = kind * STATE + source * 4 + entry
    return (column[:, None] == jnp.arange(256, dtype=jnp.int32)[None, :]).astype(bf16)


def shape(dims, kind):
    return jax.ShapeDtypeStruct(dims, kind)


PARAMS = pltpu.CompilerParams(vmem_limit_bytes=40 * 1024 * 1024)
KEEP_BYTES = 8 * 10**6
SMALL = pltpu.CompilerParams(vmem_limit_bytes=8 * 1024 * 1024)


def on_device(
    token_ids,
    accepted,
    embedding,
    norm_gain,
    w_gate,
    w_input,
    w_groups,
    w_step,
    step_bias,
    decay_rate,
    skip_gain,
    w_output,
    states,
    draft_gain,
    w_merge,
):
    x = lax.axis_index("section")
    head = lax.axis_index("head")
    y, z, c = head // 8, (head // 2) % 4, head % 2
    turned = turn_groups(w_groups[0], y, z)
    blocks = [turned[:16]] + [over_y(turned[16 * d : 16 * d + 16], d) for d in (1, 2, 3)]
    looked = pl.pallas_call(
        look_kernel,
        out_shape=shape((SLOTS, CELL), bf16),
        in_specs=[SMEM] * 2 + [pl.BlockSpec(memory_space=pl.ANY)],
        out_specs=VMEM,
        scratch_shapes=[
            pltpu.SMEM((2 * ROWS * POS,), jnp.int32),
            pltpu.VMEM((16 * PACKED, CELL), bf16),
            pltpu.SemaphoreType.DMA,
        ],
        cost_estimate=pl.CostEstimate(flops=10**9, bytes_accessed=10**7, transcendentals=0),
        compiler_params=SMALL,
        name="look",
    )(accepted, token_ids, embedding)
    looked, blocks, w_far = lax.optimization_barrier((looked, blocks, over_x(w_merge, 3)))
    found = [over_x(looked, s) for s in (1, 3, 2)]
    picked = looked.astype(f32)
    for part in found:
        picked = picked + part.astype(f32)
    picked = picked.astype(bf16)
    mine = jnp.concatenate([block[:8] for block in blocks], axis=0)
    other = jnp.concatenate([block[8:] for block in blocks], axis=0)
    pairs_half = [mine, over_z(mine, 1), over_z(other, 2), over_z(other, 3)]
    line = jnp.stack([picked] + [over_y(picked, d) for d in (1, 2, 3)])
    line, pairs_half = lax.optimization_barrier((line, pairs_half))
    pairs_half = jnp.concatenate(pairs_half, axis=0)
    w_pairs = jnp.concatenate([pairs_half, over_core(pairs_half)], axis=0)
    plane = jnp.stack([line] + [over_z(line, e) for e in (1, 2, 3)])

    pair_place = pair_places(y, z, c)
    step_columns = jnp.pad(w_step[0], ((0, 0), (0, CELL - 4)))
    plan = pl.pallas_call(
        plan_kernel,
        out_shape=(
            shape((SLOTS, SLOTS), f32),
            shape((SLOTS, SLOTS), f32),
            shape((16, SLOTS), f32),
            shape((SLOTS, STATE), jnp.int32),
        ),
        in_specs=[SMEM],
        out_specs=(VMEM,) * 4,
        compiler_params=SMALL,
        name="plan",
    )(accepted)
    start_states = states[0].reshape(ROWS, 4 * HEAD_DIM, STATE)
    pieces = (plane, over_core(plane))
    w_pair = jnp.stack([w_merge, w_far])

    saved_kinds = (
        shape((SLOTS, 4 * HEAD_DIM), bf16),
        shape((SLOTS, STATE), bf16),
        shape((16, CELL), f32),
    )
    saved = ()
    for tick in range(4):
        first, last = tick == 0, tick == 3
        part = (4, SHARE, WIDTH // 2) if last else (4, SLOTS, CHUNK)
        kinds = (
            shape((4 * SHARE if last else SLOTS, 4 * HEAD_DIM), bf16),
            shape(part[1:], bf16),
            shape(part, bf16),
        ) + saved_kinds
        if first:
            kinds = kinds + (shape((SHARE, WIDTH), bf16),)
        extra = (pair_place,) if first else saved
        gated, own, sent, *saved = pl.pallas_call(
            functools.partial(layer_kernel, first, last, tick),
            out_shape=kinds,
            in_specs=[SMEM] * 3 + [VMEM] * (13 + len(extra)),
            out_specs=(VMEM,) * len(kinds),
            scratch_shapes=[pltpu.VMEM((SLOTS, WIDTH), bf16)] * (2 if first else 1),
            compiler_params=PARAMS,
            name="layer",
        )(
            step_bias,
            decay_rate,
            skip_gain,
            *plan,
            *pieces,
            norm_gain,
            w_gate[0],
            w_input[0],
            w_pairs,
            step_columns,
            w_output[0],
            start_states,
            *extra,
        )
        if first:
            tokens = saved.pop()
            sent, w_pairs = lax.optimization_barrier((sent, w_pairs))
            w_pairs = lax.dot_general(
                w_pairs, pair_place, TN, preferred_element_type=f32
            ).astype(bf16)
        kept = pl.pallas_call(
            functools.partial(keep_kernel, last),
            out_shape=shape(part, f32),
            in_specs=[VMEM] * 3,
            out_specs=VMEM,
            compiler_params=SMALL,
            cost_estimate=pl.CostEstimate(
                flops=10**8, bytes_accessed=KEEP_BYTES, transcendentals=0
            ),
            name="keep",
        )(gated, own, w_output[0])
        other = over_core(sent)
        if last:
            other, w_pair = lax.optimization_barrier((other, w_pair))
        summed = kept + other.astype(f32)
        across = [over_z(summed[e].astype(bf16), e) for e in (1, 2, 3)]
        total = summed[0]
        for part in across:
            total = total + part.astype(f32)
        total = total.astype(bf16)
        if first:
            total, w_pairs = lax.optimization_barrier((total, w_pairs))
        if last:
            break
        arrived = [next_section(total, d) for d in range(4)]
        own = arrived[0].astype(f32)
        for part in arrived[1:]:
            own = own + part.astype(f32)
        own = own.astype(bf16)
        if tick == 2:
            own, w_pair = lax.optimization_barrier((own, w_pair))
            w_pair = over_x(w_pair, 1)
        plane = jnp.stack([own] + [over_z(own, e) for e in (1, 2, 3)])
        pieces = (plane, over_core(plane))

    kept_states = pl.pallas_call(
        state_kernel,
        out_shape=shape((ROWS, 4 * HEAD_DIM, STATE), bf16),
        in_specs=[VMEM] * 5,
        out_specs=VMEM,
        compiler_params=SMALL,
        name="kept",
    )(plan[3], *saved, start_states)

    tokens_part = pl.pallas_call(
        tokens_kernel,
        out_shape=shape((SHARE, CELL), f32),
        in_specs=[VMEM] * 4,
        out_specs=VMEM,
        compiler_params=SMALL,
        name="tokens",
    )(tokens, w_merge, w_far, w_pair)
    parts = [over_y(total, d) for d in (1, 2, 3)]
    parts, kept_states, tokens_part = lax.optimization_barrier((parts, kept_states, tokens_part))
    final = total.astype(f32)
    for part in parts:
        final = final + part.astype(f32)
    final = final.astype(bf16)
    rows = [
        route(final, lambda x, y, z, c, k=k: (z, y, z ^ k, c) if x == 3 else None)
        for k in range(4)
    ]
    rows = (rows[0] + rows[1]) + (rows[2] + rows[3])
    draft = pl.pallas_call(
        merge_kernel,
        out_shape=shape((PACKED // 4, CELL), bf16),
        in_specs=[VMEM] * 7,
        out_specs=VMEM,
        scratch_shapes=[pltpu.VMEM((SHARE, WIDTH), bf16), pltpu.VMEM((SHARE, CELL), f32)],
        compiler_params=SMALL,
        name="merge",
    )(rows, over_core(rows), tokens_part, draft_gain.reshape(1, WIDTH), w_merge, w_far, w_pair)
    return (kept_states.reshape(1, ROWS, 4, HEAD_DIM, STATE), draft)


def solution(mesh):
    return jax.shard_map(
        on_device,
        mesh=mesh,
        in_specs=(
            P(),
            P(),
            P("section", "head"),
            P("section", None),
            P("section", None, "head"),
            P("section", None, "head"),
            P("section", None, "head"),
            P("section", None, "head"),
            P("section", "head"),
            P("section", "head"),
            P("section", "head"),
            P("section", "head", None),
            P("section", None, "head", None, None),
            P(),
            P("section", "head"),
        ),
        out_specs=(P("section", None, "head", None, None), P("section", "head")),
        check_vma=False,
    )
```

```python
import functools

import jax
import jax.numpy as jnp
from jax import lax
from jax.experimental import pallas as pl
from jax.experimental.pallas import tpu as pltpu
from jax.sharding import PartitionSpec as P

HEAD_DIM = 64
STATE = 128
GROUPS = 8
ACCEPTED = 36
POS = 5
ROWS = 12
PACKED = 2 * ACCEPTED
SLOTS = 72
WIDTH = 4096
CHUNK = 512
CELL = 128
SHARE = 24

epsilon = 1e-05
bf16 = jnp.bfloat16
f32 = jnp.float32

VMEM = pl.BlockSpec(memory_space=pltpu.VMEM)
SMEM = pl.BlockSpec(memory_space=pltpu.SMEM)
NT = (((1,), (1,)), ((), ()))
TN = (((0,), (0,)), ((), ()))


def route(value, target):
    pairs = []
    for source in range(128):
        goal = target(source >> 5, (source >> 3) & 3, (source >> 1) & 3, source & 1)
        if goal is not None:
            x, y, z, c = goal
            pairs.append((source, ((x & 3) << 5) | (y << 3) | (z << 1) | c))
    return lax.ppermute(value, ("section", "head"), pairs)


def over_core(value):
    return route(value, lambda x, y, z, c: (x, y, z, c ^ 1))


def over_z(value, e):
    return route(value, lambda x, y, z, c: (x, y, z ^ e, c))


def over_y(value, d):
    return route(value, lambda x, y, z, c: (x, y ^ d, z, c))


def over_x(value, s):
    return route(value, lambda x, y, z, c: (x ^ s, y, z, c))


def next_section(value, d):
    return route(value, lambda x, y, z, c: (x + 1, y ^ d, z, c))


def coordinates():
    head = lax.axis_index("head")
    return lax.axis_index("section"), head >> 3, (head >> 1) & 3, head & 1


def ends_of(accepted_ref):
    ends = []
    for r in range(2):
        total = 0
        row = []
        for b in range(ROWS):
            total = total + accepted_ref[r, b]
            row.append(total)
        ends.append(row)
    return ends


def owner_of(ends, slot):
    later = slot >= ACCEPTED
    inner = jnp.where(later, slot - ACCEPTED, slot)
    owner = jnp.zeros_like(slot)
    for b in range(ROWS):
        end = jnp.where(later, ends[1][b], ends[0][b])
        owner = owner + (inner >= end).astype(jnp.int32)
    return owner


def look_kernel(accepted_ref, tokens_ref, table_ref, out_ref, listed, held, sem):
    ends = ends_of(accepted_ref)
    vocab_local = table_ref.shape[0]
    base = lax.axis_index("section") * vocab_local
    for r in range(2):
        for b in range(ROWS):
            start = ends[r][b] - accepted_ref[r, b] + r * ACCEPTED
            for k in range(POS):
                listed[start + k] = tokens_ref[r, b, k]
    lane = lax.broadcasted_iota(jnp.int32, (1, CELL), 1)
    slot = lax.broadcasted_iota(jnp.int32, (SLOTS, CELL), 0)
    codes = []
    for g in range(PACKED // 8):
        code = jnp.full((1, CELL), -1, jnp.int32)
        for i in range(8):
            n = 8 * g + i
            local = listed[n] - base
            row = jnp.clip(local, 0, vocab_local - 1)
            block = pl.multiple_of((row >> 4) << 4, 16)
            pltpu.make_async_copy(
                table_ref.at[pl.ds(block, 16), :], held.at[pl.ds(16 * n, 16), :], sem
            ).start()
            code = jnp.where(lane == 16 * i + (row & 15), jnp.where(local == row, n, -1), code)
        codes.append(code)
    picks = [(slot == code).astype(bf16) for code in codes]
    pltpu.make_async_copy(table_ref.at[pl.ds(0, held.shape[0]), :], held, sem).wait()
    total = jnp.zeros((SLOTS, CELL), f32)
    for g, pick in enumerate(picks):
        total = total + jnp.dot(
            pick, held[g * CELL : (g + 1) * CELL, :], preferred_element_type=f32
        )
    out_ref[...] = total.astype(bf16)


def softplus(v):
    return jnp.maximum(v, 0.0) + jnp.log1p(jnp.exp(-jnp.abs(v)))


def fill_rows(first, y, z, c, pieces, gain_ref, rows, hidden):
    total = jnp.zeros((SLOTS, CELL), f32)
    for f in range(2):
        for e in range(4):
            for d in range(4):
                if first:
                    place = ((y ^ d) * 4 + (z ^ e)) * 2 + (c ^ f)
                    part = pieces[f][e, d]
                else:
                    place = ((c ^ f) * 4 + (z ^ e)) * 4 + d
                    part = pieces[f][e, :, d * CELL : (d + 1) * CELL]
                at = pl.ds(pl.multiple_of(place * CELL, CELL), CELL)
                wide = part.astype(f32)
                total = total + wide * wide
                rows[:, at] = (wide * gain_ref[:, at]).astype(bf16)
                if first:
                    hidden[:, at] = part
    return jnp.sum(total, axis=1, keepdims=True)


def share_rows(section):
    row = lax.broadcasted_iota(jnp.int32, (SHARE, SLOTS), 0)
    slot = lax.broadcasted_iota(jnp.int32, (SHARE, SLOTS), 1)
    return ((row < PACKED // 4) & (slot == section * (PACKED // 4) + row)).astype(f32)


def plan_kernel(accepted_ref, causal_ref, after_ref, batch_ref, owner_ref):
    ends = ends_of(accepted_ref)
    slots = (SLOTS, SLOTS)
    row = lax.broadcasted_iota(jnp.int32, slots, 0)
    column = lax.broadcasted_iota(jnp.int32, slots, 1)
    same = owner_of(ends, row) == owner_of(ends, column)
    causal_ref[...] = (same & (column <= row)).astype(f32)
    after_ref[...] = (same & (column > row)).astype(f32)
    batch = lax.broadcasted_iota(jnp.int32, (16, SLOTS), 0)
    batch_owner = owner_of(ends, lax.broadcasted_iota(jnp.int32, (16, SLOTS), 1))
    batch_ref[...] = (batch == batch_owner).astype(f32)
    owner_ref[...] = owner_of(ends, lax.broadcasted_iota(jnp.int32, (SLOTS, STATE), 0))


def project(last, gated, w_output, side, z, out_ref):
    for e in range(4):
        place = side * 4 + (e if last else z ^ e)
        w = w_output[:, pl.ds(pl.multiple_of(place * CHUNK, CHUNK), CHUNK)]
        part = jnp.dot(gated, w, preferred_element_type=f32)
        if last:
            for g in range(4):
                group = part[g * SHARE : (g + 1) * SHARE].astype(out_ref.dtype)
                out_ref[g, :, e * CHUNK : (e + 1) * CHUNK] = group
        else:
            out_ref[e] = part.astype(out_ref.dtype)


def keep_kernel(last, gated_ref, own_ref, w_output, out_ref):
    _, _, z, c = coordinates()
    project(last, gated_ref[...], w_output, c, z, out_ref)
    out_ref[0] += own_ref[...].astype(f32)


def layer_kernel(first, last, tick, *refs):
    (bias_ref, rate_ref, skip_ref) = refs[:3]
    (causal_ref, after_ref, batch_ref, owner_ref) = refs[3:7]
    pieces = refs[7:9]
    (gain_ref, w_gate, w_input, w_pairs, w_step, w_output, states) = refs[9:16]
    refs = refs[16:]
    if first:
        place_ref = refs[0]
        refs = refs[1:]
    if not first:
        old_x, old_b, old_decay = refs[:3]
        refs = refs[3:]
    gated_ref, own_ref, sent_ref, new_x, new_b, new_decay = refs[:6]
    if first:
        hidden = refs[-2]
    else:
        hidden = None
    filled = refs[-1]
    x, y, z, c = coordinates()

    squares = fill_rows(first, y, z, c, pieces, gain_ref, filled, hidden)
    scale = lax.rsqrt(squares * (1.0 / WIDTH) + epsilon)
    rows = filled[...]
    if first:
        pairs = lax.dot_general(rows, w_pairs[...], NT, preferred_element_type=f32) * scale
        pairs = jnp.dot(pairs.astype(bf16), place_ref[...], preferred_element_type=f32)
    else:
        pairs = jnp.dot(rows, w_pairs[...], preferred_element_type=f32) * scale
    pairs = pairs.astype(bf16)
    b_vec, c_vec = pairs[:, :STATE], pairs[:, STATE:]
    raw = jnp.dot(rows, w_step[...], preferred_element_type=f32) * scale
    inner = jnp.dot(rows, w_input[...], preferred_element_type=f32) * scale
    gate = jnp.dot(rows, w_gate[...], preferred_element_type=f32) * scale

    lane = lax.broadcasted_iota(jnp.int32, (1, CELL), 1)
    bias = jnp.zeros((1, CELL), f32)
    rate = jnp.zeros((1, CELL), f32)
    for h in range(4):
        bias = jnp.where(lane == h, bias_ref[0, h], bias)
        rate = jnp.where(lane == h, rate_ref[0, h], rate)
    step = softplus(raw + bias)
    fall = step * rate

    causal_f32 = causal_ref[...]
    causal = causal_f32 > 0.0
    log_decay = -jnp.dot(
        causal_f32, fall, precision=lax.Precision.HIGHEST, preferred_element_type=f32
    )
    log_decay_t = -lax.dot_general(
        fall,
        causal_f32,
        (((0,), (1,)), ((), ())),
        precision=lax.Precision.HIGHEST,
        preferred_element_type=f32,
    )
    rest = -jnp.dot(
        after_ref[...], fall, precision=lax.Precision.HIGHEST, preferred_element_type=f32
    )
    total = -jnp.dot(
        batch_ref[...], fall, precision=lax.Precision.HIGHEST, preferred_element_type=f32
    )

    products = lax.dot_general(c_vec, b_vec, NT, preferred_element_type=f32)
    slot_owner = owner_ref[...]
    carried = jnp.zeros((SLOTS, 4 * HEAD_DIM), f32)
    for b in range(ROWS):
        mine = jnp.where(slot_owner == b, c_vec, jnp.zeros((), bf16))
        carried = carried + lax.dot_general(mine, states[b], NT, preferred_element_type=f32)

    wide_lane = lax.broadcasted_iota(jnp.int32, (SLOTS, 2 * HEAD_DIM), 1)
    left = wide_lane < HEAD_DIM

    def spread(v, p):
        return jnp.where(left, v[:, 2 * p : 2 * p + 1], v[:, 2 * p + 1 : 2 * p + 2])

    gated = []
    weighted = []
    for p in range(2):
        at = slice(p * 128, (p + 1) * 128)
        x_p = inner[:, at]
        dx = spread(step, p) * x_p
        dx_b = dx.astype(bf16)
        mixed = []
        for h in (2 * p, 2 * p + 1):
            gap = log_decay[:, h : h + 1] - log_decay_t[h : h + 1, :]
            weights = products * jnp.exp(jnp.where(causal, gap, -1e30))
            mixed.append(jnp.dot(weights.astype(bf16), dx_b, preferred_element_type=f32))
        out = jnp.where(left, mixed[0], mixed[1])
        out = out + jnp.exp(spread(log_decay, p)) * carried[:, at]
        skip = jnp.where(left, skip_ref[0, 2 * p], skip_ref[0, 2 * p + 1])
        out = out + skip * x_p
        g = gate[:, at]
        gated.append((out * (g / (1.0 + jnp.exp(-g)))).astype(bf16))
        weighted.append((jnp.exp(spread(rest, p)) * dx).astype(bf16))
    gated = jnp.concatenate(gated, axis=1)

    if last:
        order = jnp.concatenate([share_rows(z ^ e) for e in range(4)], axis=0).astype(bf16)
        share = share_rows(z).astype(bf16)
        gated = jnp.dot(order, gated, preferred_element_type=f32).astype(bf16)
        for k in range(4):
            own = jnp.dot(share, pieces[0][z ^ k], preferred_element_type=f32)
            own_ref[:, k * CHUNK : (k + 1) * CHUNK] = jnp.where(y == 0, own, 0.0).astype(bf16)
    else:
        if first:
            place = c * 4 + z
            own = hidden[:, pl.ds(pl.multiple_of(place * CHUNK, CHUNK), CHUNK)]
        else:
            own = pieces[0][0]
        own_ref[...] = jnp.where(y == 0, own, jnp.zeros((), bf16))
    gated_ref[...] = gated
    project(last, gated, w_output, c ^ 1, z, sent_ref)

    decay = jnp.exp(total)
    if first:
        share = share_rows(x).astype(bf16)
        refs[6][...] = jnp.dot(share, hidden[...], preferred_element_type=f32).astype(bf16)
        new_x[:, :128] = weighted[0]
        new_x[:, 128:] = weighted[1]
        new_b[...] = b_vec
        new_decay[...] = decay
    else:
        now = x == tick
        new_x[:, :128] = jnp.where(now, weighted[0], old_x[:, :128])
        new_x[:, 128:] = jnp.where(now, weighted[1], old_x[:, 128:])
        new_b[...] = jnp.where(now, b_vec, old_b[...])
        new_decay[...] = jnp.where(now, decay, old_decay[...])


def state_kernel(owner_ref, x_ref, b_ref, decay_ref, states, out_ref):
    slot_owner = owner_ref[...]
    x_all = x_ref[...]
    b_all = b_ref[...]
    for b in range(ROWS):
        mine = jnp.where(slot_owner == b, b_all, jnp.zeros((), bf16))
        added = lax.dot_general(x_all, mine, TN, preferred_element_type=f32)
        for h in range(4):
            at = slice(h * HEAD_DIM, (h + 1) * HEAD_DIM)
            scale = decay_ref[b : b + 1, h : h + 1]
            out_ref[b, at, :] = (states[b, at, :].astype(f32) * scale + added[at, :]).astype(bf16)


def add_products(x, rows, weights, low, total):
    half = WIDTH // 2
    w_own, w_far, w_pair = weights
    for way, w in ((0, w_own), (3, w_far), (1, w_pair.at[0]), (2, w_pair.at[1])):
        block = x ^ way

        @pl.when((block >= low) & (block < low + 2))
        def _():
            at = pl.ds(pl.multiple_of((block - low) * half, half), half)
            total[...] += jnp.dot(rows[:, at], w[...], preferred_element_type=f32)


def tokens_kernel(tokens_ref, *refs):
    out_ref = refs[3]
    out_ref[...] = jnp.zeros((SHARE, CELL), f32)
    add_products(lax.axis_index("section"), tokens_ref, refs[:3], 2, out_ref)


def merge_kernel(own_ref, other_ref, part_ref, gain_ref, *refs):
    out_ref, joined, total = refs[3:]
    x, _, _, c = coordinates()
    half = WIDTH // 2
    squares = jnp.zeros((SHARE, 1), f32)
    for ref in (own_ref, other_ref):
        wide = ref[...].astype(f32)
        squares = squares + jnp.sum(wide * wide, axis=1, keepdims=True)
    scale = lax.rsqrt(squares * (1.0 / WIDTH) + epsilon)
    for f, ref in enumerate((own_ref, other_ref)):
        at = pl.ds(pl.multiple_of((c ^ f) * half, half), half)
        joined[:, at] = (ref[...].astype(f32) * scale * gain_ref[:, at]).astype(bf16)
    total[...] = part_ref[...]
    add_products(x, joined, refs[:3], 0, total)
    out_ref[...] = total[: PACKED // 4, :].astype(bf16)


def turn_groups(w_groups, y, z):
    row = jnp.arange(64, dtype=jnp.int32)
    block, half, kind, entry = row // 16, (row // 8) % 2, (row // 4) % 2, row % 4
    group = (y ^ block) * 2 + ((z // 2) ^ half)
    column = (entry * 2 + kind) * 8 + group
    order = (column[:, None] == jnp.arange(64, dtype=jnp.int32)[None, :]).astype(bf16)
    return lax.dot_general(order, w_groups, NT, preferred_element_type=f32).astype(bf16)


def pair_places(y, z, c):
    row = jnp.arange(256, dtype=jnp.int32)
    f, e, d = row // 128, (row // 32) % 4, (row // 8) % 4
    kind, entry = (row // 4) % 2, row % 4
    source = ((y ^ d) * 4 + (z ^ e)) * 2 + (c ^ f)
    column = kind * STATE + source * 4 + entry
    return (column[:, None] == jnp.arange(256, dtype=jnp.int32)[None, :]).astype(bf16)


def shape(dims, kind):
    return jax.ShapeDtypeStruct(dims, kind)


PARAMS = pltpu.CompilerParams(vmem_limit_bytes=40 * 1024 * 1024)
KEEP_BYTES = 8 * 10**6
SMALL = pltpu.CompilerParams(vmem_limit_bytes=8 * 1024 * 1024)


def on_device(
    token_ids,
    accepted,
    embedding,
    norm_gain,
    w_gate,
    w_input,
    w_groups,
    w_step,
    step_bias,
    decay_rate,
    skip_gain,
    w_output,
    states,
    draft_gain,
    w_merge,
):
    x = lax.axis_index("section")
    head = lax.axis_index("head")
    y, z, c = head // 8, (head // 2) % 4, head % 2
    turned = turn_groups(w_groups[0], y, z)
    blocks = [turned[:16]] + [over_y(turned[16 * d : 16 * d + 16], d) for d in (1, 2, 3)]
    looked = pl.pallas_call(
        look_kernel,
        out_shape=shape((SLOTS, CELL), bf16),
        in_specs=[SMEM] * 2 + [pl.BlockSpec(memory_space=pl.ANY)],
        out_specs=VMEM,
        scratch_shapes=[
            pltpu.SMEM((2 * ROWS * POS,), jnp.int32),
            pltpu.VMEM((16 * PACKED, CELL), bf16),
            pltpu.SemaphoreType.DMA,
        ],
        cost_estimate=pl.CostEstimate(flops=10**9, bytes_accessed=10**7, transcendentals=0),
        compiler_params=SMALL,
        name="look",
    )(accepted, token_ids, embedding)
    looked, blocks, w_far = lax.optimization_barrier((looked, blocks, over_x(w_merge, 3)))
    found = [over_x(looked, s) for s in (1, 3, 2)]
    picked = looked.astype(f32)
    for part in found:
        picked = picked + part.astype(f32)
    picked = picked.astype(bf16)
    mine = jnp.concatenate([block[:8] for block in blocks], axis=0)
    other = jnp.concatenate([block[8:] for block in blocks], axis=0)
    pairs_half = [mine, over_z(mine, 1), over_z(other, 2), over_z(other, 3)]
    line = jnp.stack([picked] + [over_y(picked, d) for d in (1, 2, 3)])
    line, pairs_half = lax.optimization_barrier((line, pairs_half))
    pairs_half = jnp.concatenate(pairs_half, axis=0)
    w_pairs = jnp.concatenate([pairs_half, over_core(pairs_half)], axis=0)
    plane = jnp.stack([line] + [over_z(line, e) for e in (1, 2, 3)])

    pair_place = pair_places(y, z, c)
    step_columns = jnp.pad(w_step[0], ((0, 0), (0, CELL - 4)))
    plan = pl.pallas_call(
        plan_kernel,
        out_shape=(
            shape((SLOTS, SLOTS), f32),
            shape((SLOTS, SLOTS), f32),
            shape((16, SLOTS), f32),
            shape((SLOTS, STATE), jnp.int32),
        ),
        in_specs=[SMEM],
        out_specs=(VMEM,) * 4,
        compiler_params=SMALL,
        name="plan",
    )(accepted)
    start_states = states[0].reshape(ROWS, 4 * HEAD_DIM, STATE)
    pieces = (plane, over_core(plane))
    w_pair = jnp.stack([w_merge, w_far])

    saved_kinds = (
        shape((SLOTS, 4 * HEAD_DIM), bf16),
        shape((SLOTS, STATE), bf16),
        shape((16, CELL), f32),
    )
    saved = ()
    for tick in range(4):
        first, last = tick == 0, tick == 3
        part = (4, SHARE, WIDTH // 2) if last else (4, SLOTS, CHUNK)
        kinds = (
            shape((4 * SHARE if last else SLOTS, 4 * HEAD_DIM), bf16),
            shape(part[1:], bf16),
            shape(part, bf16),
        ) + saved_kinds
        if first:
            kinds = kinds + (shape((SHARE, WIDTH), bf16),)
        extra = (pair_place,) if first else saved
        gated, own, sent, *saved = pl.pallas_call(
            functools.partial(layer_kernel, first, last, tick),
            out_shape=kinds,
            in_specs=[SMEM] * 3 + [VMEM] * (13 + len(extra)),
            out_specs=(VMEM,) * len(kinds),
            scratch_shapes=[pltpu.VMEM((SLOTS, WIDTH), bf16)] * (2 if first else 1),
            compiler_params=PARAMS,
            name="layer",
        )(
            step_bias,
            decay_rate,
            skip_gain,
            *plan,
            *pieces,
            norm_gain,
            w_gate[0],
            w_input[0],
            w_pairs,
            step_columns,
            w_output[0],
            start_states,
            *extra,
        )
        if first:
            tokens = saved.pop()
            sent, w_pairs = lax.optimization_barrier((sent, w_pairs))
            w_pairs = lax.dot_general(
                w_pairs, pair_place, TN, preferred_element_type=f32
            ).astype(bf16)
        kept = pl.pallas_call(
            functools.partial(keep_kernel, last),
            out_shape=shape(part, f32),
            in_specs=[VMEM] * 3,
            out_specs=VMEM,
            compiler_params=SMALL,
            cost_estimate=pl.CostEstimate(
                flops=10**8, bytes_accessed=KEEP_BYTES, transcendentals=0
            ),
            name="keep",
        )(gated, own, w_output[0])
        other = over_core(sent)
        if last:
            other, w_pair = lax.optimization_barrier((other, w_pair))
        summed = kept + other.astype(f32)
        across = [over_z(summed[e].astype(bf16), e) for e in (1, 2, 3)]
        total = summed[0]
        for part in across:
            total = total + part.astype(f32)
        total = total.astype(bf16)
        if first:
            total, w_pairs = lax.optimization_barrier((total, w_pairs))
        if last:
            break
        arrived = [next_section(total, d) for d in range(4)]
        own = arrived[0].astype(f32)
        for part in arrived[1:]:
            own = own + part.astype(f32)
        own = own.astype(bf16)
        if tick == 2:
            own, w_pair = lax.optimization_barrier((own, w_pair))
            w_pair = over_x(w_pair, 1)
        plane = jnp.stack([own] + [over_z(own, e) for e in (1, 2, 3)])
        pieces = (plane, over_core(plane))

    kept_states = pl.pallas_call(
        state_kernel,
        out_shape=shape((ROWS, 4 * HEAD_DIM, STATE), bf16),
        in_specs=[VMEM] * 5,
        out_specs=VMEM,
        compiler_params=SMALL,
        name="kept",
    )(plan[3], *saved, start_states)

    tokens_part = pl.pallas_call(
        tokens_kernel,
        out_shape=shape((SHARE, CELL), f32),
        in_specs=[VMEM] * 4,
        out_specs=VMEM,
        compiler_params=SMALL,
        name="tokens",
    )(tokens, w_merge, w_far, w_pair)
    parts = [over_y(total, d) for d in (1, 2, 3)]
    parts, kept_states, tokens_part = lax.optimization_barrier((parts, kept_states, tokens_part))
    final = total.astype(f32)
    for part in parts:
        final = final + part.astype(f32)
    final = final.astype(bf16)
    rows = [
        route(final, lambda x, y, z, c, k=k: (z, y, z ^ k, c) if x == 3 else None)
        for k in range(4)
    ]
    rows = (rows[0] + rows[1]) + (rows[2] + rows[3])
    draft = pl.pallas_call(
        merge_kernel,
        out_shape=shape((PACKED // 4, CELL), bf16),
        in_specs=[VMEM] * 7,
        out_specs=VMEM,
        scratch_shapes=[pltpu.VMEM((SHARE, WIDTH), bf16), pltpu.VMEM((SHARE, CELL), f32)],
        compiler_params=SMALL,
        name="merge",
    )(rows, over_core(rows), tokens_part, draft_gain.reshape(1, WIDTH), w_merge, w_far, w_pair)
    return (kept_states.reshape(1, ROWS, 4, HEAD_DIM, STATE), draft)


def solution(mesh):
    return jax.shard_map(
        on_device,
        mesh=mesh,
        in_specs=(
            P(),
            P(),
            P("section", "head"),
            P("section", None),
            P("section", None, "head"),
            P("section", None, "head"),
            P("section", None, "head"),
            P("section", None, "head"),
            P("section", "head"),
            P("section", "head"),
            P("section", "head"),
            P("section", "head", None),
            P("section", None, "head", None, None),
            P(),
            P("section", "head"),
        ),
        out_specs=(P("section", None, "head", None, None), P("section", "head")),
        check_vma=False,
    )
```

```python
import functools

import jax
import jax.numpy as jnp
from jax import lax
from jax.experimental import pallas as pl
from jax.experimental.pallas import tpu as pltpu
from jax.sharding import PartitionSpec as P

HEAD_DIM = 64
STATE = 128
GROUPS = 8
ACCEPTED = 36
POS = 5
ROWS = 12
PACKED = 2 * ACCEPTED
SLOTS = 72
WIDTH = 4096
CHUNK = 512
CELL = 128
SHARE = 24

epsilon = 1e-05
bf16 = jnp.bfloat16
f32 = jnp.float32

VMEM = pl.BlockSpec(memory_space=pltpu.VMEM)
SMEM = pl.BlockSpec(memory_space=pltpu.SMEM)
NT = (((1,), (1,)), ((), ()))
TN = (((0,), (0,)), ((), ()))


def route(value, target):
    pairs = []
    for source in range(128):
        goal = target(source >> 5, (source >> 3) & 3, (source >> 1) & 3, source & 1)
        if goal is not None:
            x, y, z, c = goal
            pairs.append((source, ((x & 3) << 5) | (y << 3) | (z << 1) | c))
    return lax.ppermute(value, ("section", "head"), pairs)


def over_core(value):
    return route(value, lambda x, y, z, c: (x, y, z, c ^ 1))


def over_z(value, e):
    return route(value, lambda x, y, z, c: (x, y, z ^ e, c))


def over_y(value, d):
    return route(value, lambda x, y, z, c: (x, y ^ d, z, c))


def over_x(value, s):
    return route(value, lambda x, y, z, c: (x ^ s, y, z, c))


def next_section(value, d):
    return route(value, lambda x, y, z, c: (x + 1, y ^ d, z, c))


def coordinates():
    head = lax.axis_index("head")
    return lax.axis_index("section"), head >> 3, (head >> 1) & 3, head & 1


def ends_of(accepted_ref):
    ends = []
    for r in range(2):
        total = 0
        row = []
        for b in range(ROWS):
            total = total + accepted_ref[r, b]
            row.append(total)
        ends.append(row)
    return ends


def owner_of(ends, slot):
    later = slot >= ACCEPTED
    inner = jnp.where(later, slot - ACCEPTED, slot)
    owner = jnp.zeros_like(slot)
    for b in range(ROWS):
        end = jnp.where(later, ends[1][b], ends[0][b])
        owner = owner + (inner >= end).astype(jnp.int32)
    return owner


def look_kernel(accepted_ref, tokens_ref, table_ref, out_ref, listed, held, sem):
    ends = ends_of(accepted_ref)
    vocab_local = table_ref.shape[0]
    base = lax.axis_index("section") * vocab_local
    for r in range(2):
        for b in range(ROWS):
            start = ends[r][b] - accepted_ref[r, b] + r * ACCEPTED
            for k in range(POS):
                listed[start + k] = tokens_ref[r, b, k]
    lane = lax.broadcasted_iota(jnp.int32, (1, CELL), 1)
    slot = lax.broadcasted_iota(jnp.int32, (SLOTS, CELL), 0)
    codes = []
    for g in range(PACKED // 8):
        code = jnp.full((1, CELL), -1, jnp.int32)
        for i in range(8):
            n = 8 * g + i
            local = listed[n] - base
            row = jnp.clip(local, 0, vocab_local - 1)
            block = pl.multiple_of((row >> 4) << 4, 16)
            pltpu.make_async_copy(
                table_ref.at[pl.ds(block, 16), :], held.at[pl.ds(16 * n, 16), :], sem
            ).start()
            code = jnp.where(lane == 16 * i + (row & 15), jnp.where(local == row, n, -1), code)
        codes.append(code)
    picks = [(slot == code).astype(bf16) for code in codes]
    pltpu.make_async_copy(table_ref.at[pl.ds(0, held.shape[0]), :], held, sem).wait()
    total = jnp.zeros((SLOTS, CELL), f32)
    for g, pick in enumerate(picks):
        total = total + jnp.dot(
            pick, held[g * CELL : (g + 1) * CELL, :], preferred_element_type=f32
        )
    out_ref[...] = total.astype(bf16)


def softplus(v):
    return jnp.maximum(v, 0.0) + jnp.log1p(jnp.exp(-jnp.abs(v)))


def fill_rows(first, y, z, c, pieces, gain_ref, rows, hidden):
    total = jnp.zeros((SLOTS, CELL), f32)
    for f in range(2):
        for e in range(4):
            for d in range(4):
                if first:
                    place = ((y ^ d) * 4 + (z ^ e)) * 2 + (c ^ f)
                    part = pieces[f][e, d]
                else:
                    place = ((c ^ f) * 4 + (z ^ e)) * 4 + d
                    part = pieces[f][e, :, d * CELL : (d + 1) * CELL]
                at = pl.ds(pl.multiple_of(place * CELL, CELL), CELL)
                wide = part.astype(f32)
                total = total + wide * wide
                rows[:, at] = (wide * gain_ref[:, at]).astype(bf16)
                if first:
                    hidden[:, at] = part
    return jnp.sum(total, axis=1, keepdims=True)


def share_rows(section):
    row = lax.broadcasted_iota(jnp.int32, (SHARE, SLOTS), 0)
    slot = lax.broadcasted_iota(jnp.int32, (SHARE, SLOTS), 1)
    return ((row < PACKED // 4) & (slot == section * (PACKED // 4) + row)).astype(f32)


def plan_kernel(accepted_ref, causal_ref, after_ref, batch_ref, owner_ref):
    ends = ends_of(accepted_ref)
    slots = (SLOTS, SLOTS)
    row = lax.broadcasted_iota(jnp.int32, slots, 0)
    column = lax.broadcasted_iota(jnp.int32, slots, 1)
    same = owner_of(ends, row) == owner_of(ends, column)
    causal_ref[...] = (same & (column <= row)).astype(f32)
    after_ref[...] = (same & (column > row)).astype(f32)
    batch = lax.broadcasted_iota(jnp.int32, (16, SLOTS), 0)
    batch_owner = owner_of(ends, lax.broadcasted_iota(jnp.int32, (16, SLOTS), 1))
    batch_ref[...] = (batch == batch_owner).astype(f32)
    owner_ref[...] = owner_of(ends, lax.broadcasted_iota(jnp.int32, (SLOTS, STATE), 0))


def project(last, gated, w_output, side, z, out_ref):
    for e in range(4):
        place = side * 4 + (e if last else z ^ e)
        w = w_output[:, pl.ds(pl.multiple_of(place * CHUNK, CHUNK), CHUNK)]
        part = jnp.dot(gated, w, preferred_element_type=f32)
        if last:
            for g in range(4):
                group = part[g * SHARE : (g + 1) * SHARE].astype(out_ref.dtype)
                out_ref[g, :, e * CHUNK : (e + 1) * CHUNK] = group
        else:
            out_ref[e] = part.astype(out_ref.dtype)


def keep_kernel(last, gated_ref, own_ref, w_output, out_ref):
    _, _, z, c = coordinates()
    project(last, gated_ref[...], w_output, c, z, out_ref)
    out_ref[0] += own_ref[...].astype(f32)


def layer_kernel(first, last, tick, *refs):
    (bias_ref, rate_ref, skip_ref) = refs[:3]
    (causal_ref, after_ref, batch_ref, owner_ref) = refs[3:7]
    pieces = refs[7:9]
    (gain_ref, w_gate, w_input, w_pairs, w_step, w_output, states) = refs[9:16]
    refs = refs[16:]
    if first:
        place_ref = refs[0]
        refs = refs[1:]
    if not first:
        old_x, old_b, old_decay = refs[:3]
        refs = refs[3:]
    gated_ref, own_ref, sent_ref, new_x, new_b, new_decay = refs[:6]
    if first:
        hidden = refs[-2]
    else:
        hidden = None
    filled = refs[-1]
    x, y, z, c = coordinates()

    squares = fill_rows(first, y, z, c, pieces, gain_ref, filled, hidden)
    scale = lax.rsqrt(squares * (1.0 / WIDTH) + epsilon)
    rows = filled[...]
    if first:
        pairs = jnp.dot(rows, w_pairs[...], preferred_element_type=f32) * scale
        pairs = jnp.dot(pairs.astype(bf16), place_ref[...], preferred_element_type=f32)
    else:
        pairs = jnp.dot(rows, w_pairs[...], preferred_element_type=f32) * scale
    pairs = pairs.astype(bf16)
    b_vec, c_vec = pairs[:, :STATE], pairs[:, STATE:]
    raw = jnp.dot(rows, w_step[...], preferred_element_type=f32) * scale
    inner = jnp.dot(rows, w_input[...], preferred_element_type=f32) * scale
    gate = jnp.dot(rows, w_gate[...], preferred_element_type=f32) * scale

    lane = lax.broadcasted_iota(jnp.int32, (1, CELL), 1)
    bias = jnp.zeros((1, CELL), f32)
    rate = jnp.zeros((1, CELL), f32)
    for h in range(4):
        bias = jnp.where(lane == h, bias_ref[0, h], bias)
        rate = jnp.where(lane == h, rate_ref[0, h], rate)
    step = softplus(raw + bias)
    fall = step * rate

    causal_f32 = causal_ref[...]
    causal = causal_f32 > 0.0
    log_decay = -jnp.dot(
        causal_f32, fall, precision=lax.Precision.HIGHEST, preferred_element_type=f32
    )
    log_decay_t = -lax.dot_general(
        fall,
        causal_f32,
        (((0,), (1,)), ((), ())),
        precision=lax.Precision.HIGHEST,
        preferred_element_type=f32,
    )
    rest = -jnp.dot(
        after_ref[...], fall, precision=lax.Precision.HIGHEST, preferred_element_type=f32
    )
    total = -jnp.dot(
        batch_ref[...], fall, precision=lax.Precision.HIGHEST, preferred_element_type=f32
    )

    products = lax.dot_general(c_vec, b_vec, NT, preferred_element_type=f32)
    slot_owner = owner_ref[...]
    carried = jnp.zeros((SLOTS, 4 * HEAD_DIM), f32)
    for b in range(ROWS):
        mine = jnp.where(slot_owner == b, c_vec, jnp.zeros((), bf16))
        carried = carried + lax.dot_general(mine, states[b], NT, preferred_element_type=f32)

    wide_lane = lax.broadcasted_iota(jnp.int32, (SLOTS, 2 * HEAD_DIM), 1)
    left = wide_lane < HEAD_DIM

    def spread(v, p):
        return jnp.where(left, v[:, 2 * p : 2 * p + 1], v[:, 2 * p + 1 : 2 * p + 2])

    gated = []
    weighted = []
    for p in range(2):
        at = slice(p * 128, (p + 1) * 128)
        x_p = inner[:, at]
        dx = spread(step, p) * x_p
        dx_b = dx.astype(bf16)
        mixed = []
        for h in (2 * p, 2 * p + 1):
            gap = log_decay[:, h : h + 1] - log_decay_t[h : h + 1, :]
            weights = products * jnp.exp(jnp.where(causal, gap, -1e30))
            mixed.append(jnp.dot(weights.astype(bf16), dx_b, preferred_element_type=f32))
        out = jnp.where(left, mixed[0], mixed[1])
        out = out + jnp.exp(spread(log_decay, p)) * carried[:, at]
        skip = jnp.where(left, skip_ref[0, 2 * p], skip_ref[0, 2 * p + 1])
        out = out + skip * x_p
        g = gate[:, at]
        gated.append((out * (g / (1.0 + jnp.exp(-g)))).astype(bf16))
        weighted.append((jnp.exp(spread(rest, p)) * dx).astype(bf16))
    gated = jnp.concatenate(gated, axis=1)

    if last:
        order = jnp.concatenate([share_rows(z ^ e) for e in range(4)], axis=0).astype(bf16)
        share = share_rows(z).astype(bf16)
        gated = jnp.dot(order, gated, preferred_element_type=f32).astype(bf16)
        for k in range(4):
            own = jnp.dot(share, pieces[0][z ^ k], preferred_element_type=f32)
            own_ref[:, k * CHUNK : (k + 1) * CHUNK] = jnp.where(y == 0, own, 0.0).astype(bf16)
    else:
        if first:
            place = c * 4 + z
            own = hidden[:, pl.ds(pl.multiple_of(place * CHUNK, CHUNK), CHUNK)]
        else:
            own = pieces[0][0]
        own_ref[...] = jnp.where(y == 0, own, jnp.zeros((), bf16))
    gated_ref[...] = gated
    project(last, gated, w_output, c ^ 1, z, sent_ref)

    decay = jnp.exp(total)
    if first:
        share = share_rows(x).astype(bf16)
        refs[6][...] = jnp.dot(share, hidden[...], preferred_element_type=f32).astype(bf16)
        new_x[:, :128] = weighted[0]
        new_x[:, 128:] = weighted[1]
        new_b[...] = b_vec
        new_decay[...] = decay
    else:
        now = x == tick
        new_x[:, :128] = jnp.where(now, weighted[0], old_x[:, :128])
        new_x[:, 128:] = jnp.where(now, weighted[1], old_x[:, 128:])
        new_b[...] = jnp.where(now, b_vec, old_b[...])
        new_decay[...] = jnp.where(now, decay, old_decay[...])


def state_kernel(owner_ref, x_ref, b_ref, decay_ref, states, out_ref):
    slot_owner = owner_ref[...]
    x_all = x_ref[...]
    b_all = b_ref[...]
    for b in range(ROWS):
        mine = jnp.where(slot_owner == b, b_all, jnp.zeros((), bf16))
        added = lax.dot_general(x_all, mine, TN, preferred_element_type=f32)
        for h in range(4):
            at = slice(h * HEAD_DIM, (h + 1) * HEAD_DIM)
            scale = decay_ref[b : b + 1, h : h + 1]
            out_ref[b, at, :] = (states[b, at, :].astype(f32) * scale + added[at, :]).astype(bf16)


def add_products(x, rows, weights, low, total):
    half = WIDTH // 2
    w_own, w_far, w_pair = weights
    for way, w in ((0, w_own), (3, w_far), (1, w_pair.at[0]), (2, w_pair.at[1])):
        block = x ^ way

        @pl.when((block >= low) & (block < low + 2))
        def _():
            at = pl.ds(pl.multiple_of((block - low) * half, half), half)
            total[...] += jnp.dot(rows[:, at], w[...], preferred_element_type=f32)


def tokens_kernel(tokens_ref, *refs):
    out_ref = refs[3]
    out_ref[...] = jnp.zeros((SHARE, CELL), f32)
    add_products(lax.axis_index("section"), tokens_ref, refs[:3], 2, out_ref)


def merge_kernel(own_ref, other_ref, part_ref, gain_ref, *refs):
    out_ref, joined, total = refs[3:]
    x, _, _, c = coordinates()
    half = WIDTH // 2
    squares = jnp.zeros((SHARE, 1), f32)
    for ref in (own_ref, other_ref):
        wide = ref[...].astype(f32)
        squares = squares + jnp.sum(wide * wide, axis=1, keepdims=True)
    scale = lax.rsqrt(squares * (1.0 / WIDTH) + epsilon)
    for f, ref in enumerate((own_ref, other_ref)):
        at = pl.ds(pl.multiple_of((c ^ f) * half, half), half)
        joined[:, at] = (ref[...].astype(f32) * scale * gain_ref[:, at]).astype(bf16)
    total[...] = part_ref[...]
    add_products(x, joined, refs[:3], 0, total)
    out_ref[...] = total[: PACKED // 4, :].astype(bf16)


def turn_groups(w_groups, y, z):
    row = jnp.arange(64, dtype=jnp.int32)
    block, half, kind, entry = row // 16, (row // 8) % 2, (row // 4) % 2, row % 4
    group = (y ^ block) * 2 + ((z // 2) ^ half)
    column = (entry * 2 + kind) * 8 + group
    order = (column[:, None] == jnp.arange(64, dtype=jnp.int32)[None, :]).astype(bf16)
    return lax.dot_general(order, w_groups, NT, preferred_element_type=f32).astype(bf16)


def pair_places(y, z, c):
    row = jnp.arange(256, dtype=jnp.int32)
    f, e, d = row // 128, (row // 32) % 4, (row // 8) % 4
    kind, entry = (row // 4) % 2, row % 4
    source = ((y ^ d) * 4 + (z ^ e)) * 2 + (c ^ f)
    column = kind * STATE + source * 4 + entry
    return (column[:, None] == jnp.arange(256, dtype=jnp.int32)[None, :]).astype(bf16)


def shape(dims, kind):
    return jax.ShapeDtypeStruct(dims, kind)


PARAMS = pltpu.CompilerParams(vmem_limit_bytes=40 * 1024 * 1024)
KEEP_BYTES = 8 * 10**6
SMALL = pltpu.CompilerParams(vmem_limit_bytes=8 * 1024 * 1024)


def on_device(
    token_ids,
    accepted,
    embedding,
    norm_gain,
    w_gate,
    w_input,
    w_groups,
    w_step,
    step_bias,
    decay_rate,
    skip_gain,
    w_output,
    states,
    draft_gain,
    w_merge,
):
    x = lax.axis_index("section")
    head = lax.axis_index("head")
    y, z, c = head // 8, (head // 2) % 4, head % 2
    turned = turn_groups(w_groups[0], y, z)
    blocks = [turned[:16]] + [over_y(turned[16 * d : 16 * d + 16], d) for d in (1, 2, 3)]
    looked = pl.pallas_call(
        look_kernel,
        out_shape=shape((SLOTS, CELL), bf16),
        in_specs=[SMEM] * 2 + [pl.BlockSpec(memory_space=pl.ANY)],
        out_specs=VMEM,
        scratch_shapes=[
            pltpu.SMEM((2 * ROWS * POS,), jnp.int32),
            pltpu.VMEM((16 * PACKED, CELL), bf16),
            pltpu.SemaphoreType.DMA,
        ],
        cost_estimate=pl.CostEstimate(flops=10**9, bytes_accessed=10**7, transcendentals=0),
        compiler_params=SMALL,
        name="look",
    )(accepted, token_ids, embedding)
    looked, blocks, w_far = lax.optimization_barrier((looked, blocks, over_x(w_merge, 3)))
    found = [over_x(looked, s) for s in (1, 3, 2)]
    picked = looked.astype(f32)
    for part in found:
        picked = picked + part.astype(f32)
    picked = picked.astype(bf16)
    mine = jnp.concatenate([block[:8] for block in blocks], axis=0)
    other = jnp.concatenate([block[8:] for block in blocks], axis=0)
    pairs_half = [mine, over_z(mine, 1), over_z(other, 2), over_z(other, 3)]
    line = jnp.stack([picked] + [over_y(picked, d) for d in (1, 2, 3)])
    line, pairs_half = lax.optimization_barrier((line, pairs_half))
    pairs_half = jnp.concatenate(pairs_half, axis=0).T
    w_pairs = jnp.concatenate([pairs_half, over_core(pairs_half)], axis=1)
    plane = jnp.stack([line] + [over_z(line, e) for e in (1, 2, 3)])

    pair_place = pair_places(y, z, c)
    step_columns = jnp.pad(w_step[0], ((0, 0), (0, CELL - 4)))
    plan = pl.pallas_call(
        plan_kernel,
        out_shape=(
            shape((SLOTS, SLOTS), f32),
            shape((SLOTS, SLOTS), f32),
            shape((16, SLOTS), f32),
            shape((SLOTS, STATE), jnp.int32),
        ),
        in_specs=[SMEM],
        out_specs=(VMEM,) * 4,
        compiler_params=SMALL,
        name="plan",
    )(accepted)
    start_states = states[0].reshape(ROWS, 4 * HEAD_DIM, STATE)
    pieces = (plane, over_core(plane))
    w_pair = jnp.stack([w_merge, w_far])

    saved_kinds = (
        shape((SLOTS, 4 * HEAD_DIM), bf16),
        shape((SLOTS, STATE), bf16),
        shape((16, CELL), f32),
    )
    saved = ()
    for tick in range(4):
        first, last = tick == 0, tick == 3
        part = (4, SHARE, WIDTH // 2) if last else (4, SLOTS, CHUNK)
        kinds = (
            shape((4 * SHARE if last else SLOTS, 4 * HEAD_DIM), bf16),
            shape(part[1:], bf16),
            shape(part, bf16),
        ) + saved_kinds
        if first:
            kinds = kinds + (shape((SHARE, WIDTH), bf16),)
        extra = (pair_place,) if first else saved
        gated, own, sent, *saved = pl.pallas_call(
            functools.partial(layer_kernel, first, last, tick),
            out_shape=kinds,
            in_specs=[SMEM] * 3 + [VMEM] * (13 + len(extra)),
            out_specs=(VMEM,) * len(kinds),
            scratch_shapes=[pltpu.VMEM((SLOTS, WIDTH), bf16)] * (2 if first else 1),
            compiler_params=PARAMS,
            name="layer",
        )(
            step_bias,
            decay_rate,
            skip_gain,
            *plan,
            *pieces,
            norm_gain,
            w_gate[0],
            w_input[0],
            w_pairs,
            step_columns,
            w_output[0],
            start_states,
            *extra,
        )
        if first:
            tokens = saved.pop()
            sent, w_pairs = lax.optimization_barrier((sent, w_pairs))
            w_pairs = jnp.dot(w_pairs, pair_place, preferred_element_type=f32).astype(bf16)
        kept = pl.pallas_call(
            functools.partial(keep_kernel, last),
            out_shape=shape(part, f32),
            in_specs=[VMEM] * 3,
            out_specs=VMEM,
            compiler_params=SMALL,
            cost_estimate=pl.CostEstimate(
                flops=10**8, bytes_accessed=KEEP_BYTES, transcendentals=0
            ),
            name="keep",
        )(gated, own, w_output[0])
        other = over_core(sent)
        if last:
            other, w_pair = lax.optimization_barrier((other, w_pair))
        summed = kept + other.astype(f32)
        across = [over_z(summed[e].astype(bf16), e) for e in (1, 2, 3)]
        total = summed[0]
        for part in across:
            total = total + part.astype(f32)
        total = total.astype(bf16)
        if first:
            total, w_pairs = lax.optimization_barrier((total, w_pairs))
        if last:
            break
        arrived = [next_section(total, d) for d in range(4)]
        own = arrived[0].astype(f32)
        for part in arrived[1:]:
            own = own + part.astype(f32)
        own = own.astype(bf16)
        if tick == 2:
            own, w_pair = lax.optimization_barrier((own, w_pair))
            w_pair = over_x(w_pair, 1)
        plane = jnp.stack([own] + [over_z(own, e) for e in (1, 2, 3)])
        pieces = (plane, over_core(plane))

    kept_states = pl.pallas_call(
        state_kernel,
        out_shape=shape((ROWS, 4 * HEAD_DIM, STATE), bf16),
        in_specs=[VMEM] * 5,
        out_specs=VMEM,
        compiler_params=SMALL,
        name="kept",
    )(plan[3], *saved, start_states)

    tokens_part = pl.pallas_call(
        tokens_kernel,
        out_shape=shape((SHARE, CELL), f32),
        in_specs=[VMEM] * 4,
        out_specs=VMEM,
        compiler_params=SMALL,
        name="tokens",
    )(tokens, w_merge, w_far, w_pair)
    parts = [over_y(total, d) for d in (1, 2, 3)]
    parts, kept_states, tokens_part = lax.optimization_barrier((parts, kept_states, tokens_part))
    final = total.astype(f32)
    for part in parts:
        final = final + part.astype(f32)
    final = final.astype(bf16)
    rows = [
        route(final, lambda x, y, z, c, k=k: (z, y, z ^ k, c) if x == 3 else None)
        for k in range(4)
    ]
    rows = (rows[0] + rows[1]) + (rows[2] + rows[3])
    draft = pl.pallas_call(
        merge_kernel,
        out_shape=shape((PACKED // 4, CELL), bf16),
        in_specs=[VMEM] * 7,
        out_specs=VMEM,
        scratch_shapes=[pltpu.VMEM((SHARE, WIDTH), bf16), pltpu.VMEM((SHARE, CELL), f32)],
        compiler_params=SMALL,
        name="merge",
    )(rows, over_core(rows), tokens_part, draft_gain.reshape(1, WIDTH), w_merge, w_far, w_pair)
    return (kept_states.reshape(1, ROWS, 4, HEAD_DIM, STATE), draft)


def solution(mesh):
    return jax.shard_map(
        on_device,
        mesh=mesh,
        in_specs=(
            P(),
            P(),
            P("section", "head"),
            P("section", None),
            P("section", None, "head"),
            P("section", None, "head"),
            P("section", None, "head"),
            P("section", None, "head"),
            P("section", "head"),
            P("section", "head"),
            P("section", "head"),
            P("section", "head", None),
            P("section", None, "head", None, None),
            P(),
            P("section", "head"),
        ),
        out_specs=(P("section", None, "head", None, None), P("section", "head")),
        check_vma=False,
    )
```
